256 devices in a mesh: row: 8 (over x, core), axial: 32 (over z, y).
Axes of the slice: x: 4, y: 4, z: 8, core: 2. Of those that a mesh axis runs over, the one named last changes fastest.
Arguments:
- prior_warmth: float32 [1024, 128, 256], P('axial', 'row'), may hold values from -6 to 6
- tube_supply: float32 [1024, 128, 256], P('axial', 'row'), may hold values from -6 to 7
- lower_coupling: float32 [1024, 128, 256], P('axial', 'row'), may hold values from 4096 to 32768
- higher_coupling: float32 [1024, 128, 256], P('axial', 'row'), may hold values from 4096 to 32768
- void_ratio: float32 [4], replicated, may hold values from 0.1 to 1
- void_group: int32 [128, 256], P('row'), may hold values from 0 to 3
- baffle_region: int32 [1024], P('axial'), may hold values from 0 to 31, never falling along the last dimension, each value on 1 to 64 neighbouring positions
- transverse_sense: int32 [32], replicated, may hold values from 0 to 1
Outputs:
- temperature_new: float32 [1024, 128, 256], P('axial', 'row')
The draws below stay inside these ranges and needn't reach their ends.
Inputs may be any that keep to these rules, and one draw needn't show every extreme that they name: `baffle_region`: zone ids never fall along the axial dimension; every zone holds at least one slab.
All inputs are finite; a program needn't handle non-finite values.
Results may differ from the reference program's by a relative error of at most 0.0011.
Values sent between devices are 32-bit elements; how exact they have to be, the bound alone decides.
A program may use at most 64 MiB of HBM per device.

```python
import math
import jax
import jax.numpy as jnp
import numpy as np
from jax import lax

NCLASS = 4
NZONE = 32
NX = 128
NY = 256
NZ = 1024


def draw_prior_warmth(key, part):
    first_key, second_key = jax.random.split(jax.random.fold_in(key, 11))
    line_part = jnp.clip(jax.random.normal(first_key, (NX, NY), jnp.float32), -4.0, 4.0)
    rough_part = jnp.clip(0.5 * jax.random.normal(second_key, (NZ, NX, NY), jnp.float32), -2.0, 2.0)
    return line_part[None] + rough_part


def draw_tube_supply(key, part):
    first_key, second_key = jax.random.split(jax.random.fold_in(key, 23))
    line_part = jnp.clip(jax.random.normal(first_key, (NX, NY), jnp.float32), -4.0, 4.0)
    rough_part = jnp.clip(0.5 * jax.random.normal(second_key, (NZ, NX, NY), jnp.float32), -2.0, 2.0)
    return line_part[None] + rough_part


def with_ends(entries, own_key, smallest, high):
    spot = [jax.random.randint(jax.random.fold_in(own_key, axis), (), 0, length) for axis, length in enumerate(entries.shape)]
    widest = entries.shape.index(max(entries.shape))
    neighbour = spot[:widest] + [(spot[widest] + 1) % entries.shape[widest]] + spot[widest + 1:]
    return entries.at[tuple(spot)].set(smallest).at[tuple(neighbour)].set(high)


def level_of(key, dims, cuts, smallest, top_value):
    gain = 1.0
    for axis_at, shards_of in cuts:
        steps = jax.random.uniform(jax.random.fold_in(jax.random.fold_in(key, 6), axis_at), (shards_of,), jnp.float32, smallest / len(cuts), top_value / len(cuts))
        gain = gain * jnp.repeat(jnp.exp(steps), dims[axis_at] // shards_of).reshape((-1,) + (1,) * (len(dims) - 1 - axis_at))
    return gain


def profile(count, total, reach, lean):
    portions = [(1 << 20) // math.isqrt(rank ** lean) + 1 for rank in range(2, count + 1)]
    rest, counts = total - reach - (count - 1), [1] * (count - 1)
    while rest > 0:
        movable = [i for i in range(count - 1) if counts[i] < reach]
        pool, budget = sum([portions[i] for i in movable]), rest
        for i in movable:
            addition = min(reach - counts[i], max(1, budget * portions[i] // pool), rest)
            counts[i] = counts[i] + addition
            rest = rest - addition
    return np.array([reach] + counts)


def ragged(rng, count, total, bound, lean):
    if count == 2:
        one = jax.random.randint(rng, (), max(1, total - bound), min(bound, total - 1) + 1)
        return jnp.stack([one, total - one])
    lengths = jnp.asarray(profile(count, total, bound, lean), jnp.int32)
    couples = (count - 1) // 2
    source_of, taker = lengths[1:1 + 2 * couples:2], lengths[2:2 + 2 * couples:2]
    room = jnp.minimum(source_of - 1, bound - taker)
    moved = jax.random.randint(jax.random.fold_in(rng, 1), (couples,), 0, 1 << 20) % (room + 1)
    lengths = lengths.at[1:1 + 2 * couples:2].set(source_of - moved).at[2:2 + 2 * couples:2].set(taker + moved)
    return lengths[jax.random.permutation(jax.random.fold_in(rng, 2), count)]


def setup_inputs(seed: int = 0) -> dict:
    key_list = jax.random.split(jax.random.key(seed), 9)
    prior_warmth = draw_prior_warmth(jax.random.fold_in(key_list[8], 71), 0)
    tube_supply = draw_tube_supply(jax.random.fold_in(key_list[8], 71), 0)
    lower_coupling = jnp.clip(jnp.exp(math.log(32768.0) - 2.0794415 * jax.random.uniform(key_list[2], (NZ, NX, NY), jnp.float32) ** level_of(key_list[2], (NZ, NX, NY), ((0, 32), (1, 8)), -0.2, 0.2)), 4096.0, 32768.0)
    higher_coupling = jnp.clip(jnp.exp(math.log(32768.0) - 2.0794415 * jax.random.uniform(key_list[3], (NZ, NX, NY), jnp.float32) ** level_of(key_list[3], (NZ, NX, NY), ((0, 32), (1, 8)), -0.2, 0.2)), 4096.0, 32768.0)
    void_ratio = jnp.clip(jax.random.uniform(key_list[4], (NCLASS,), jnp.float32, 0.1, 1.0), 0.1, 1.0)
    void_group = with_ends(jax.random.randint(key_list[5], (NX, NY), 0, NCLASS), jax.random.fold_in(key_list[5], 1), 0, NCLASS - 1).astype(jnp.int32)
    baffle_region = jnp.searchsorted(jnp.cumsum(ragged(key_list[6], NZONE, NZ, 2 * NZ // NZONE, 0)), jnp.arange(NZ), side="right").astype(jnp.int32)
    transverse_sense = with_ends(jax.random.randint(key_list[7], (NZONE,), 0, 2), jax.random.fold_in(key_list[7], 1), 0, 1).astype(jnp.int32)
    return {"prior_warmth": prior_warmth, "tube_supply": tube_supply, "lower_coupling": lower_coupling, "higher_coupling": higher_coupling, "void_ratio": void_ratio, "void_group": void_group, "baffle_region": baffle_region, "transverse_sense": transverse_sense}


transverse_speed = 0.35
mixing_coefficient = 0.15
supplied_power = 0.5
axial_drift = 64.0


def sweep(state_pair, inputs):
    gain_prev, value_prev = state_pair
    lower_band, main_band, upper_band, lagged_contribution = inputs
    pivot_now = main_band - lower_band * gain_prev
    gain_now = upper_band / pivot_now
    value_now = (lagged_contribution + lower_band * value_prev) / pivot_now
    return (gain_now, value_now), (gain_now, value_now)


def back_step(above_value, inputs):
    gain_now, value_now = inputs
    level_now = value_now + gain_now * above_value
    return level_now, level_now


def reference(prior_warmth, tube_supply, lower_coupling, higher_coupling, void_ratio, void_group, baffle_region, transverse_sense):
    void_share = void_ratio[void_group]
    elimination_sweep = transverse_sense[baffle_region].astype(jnp.float32)[:, None, None]
    sideways_margin = jnp.pad(prior_warmth, ((0, 0), (1, 1), (1, 1)))
    leftside_boundary = sideways_margin[:, :-2, 1:-1]
    right_boundary = sideways_margin[:, 2:, 1:-1]
    bottom_boundary = sideways_margin[:, 1:-1, :-2]
    upper_boundary = sideways_margin[:, 1:-1, 2:]
    lagged_contribution = prior_warmth + transverse_speed * void_share * (elimination_sweep * (leftside_boundary - prior_warmth) + (1.0 - elimination_sweep) * (right_boundary - prior_warmth)) + mixing_coefficient * (leftside_boundary + right_boundary + bottom_boundary + upper_boundary - 4.0 * prior_warmth) + supplied_power * tube_supply
    lower_band = lower_coupling + axial_drift
    main_band = 1.0 + lower_coupling + higher_coupling + axial_drift
    blank_layer = jnp.zeros(prior_warmth.shape[1:], jnp.float32)
    unused, (gains, values) = lax.scan(sweep, (blank_layer, blank_layer), (lower_band, main_band, higher_coupling, lagged_contribution))
    unused_top, updated = lax.scan(back_step, blank_layer, (gains, values), reverse=True)
    return updated
```

```python
import functools

import jax
import jax.numpy as jnp
from jax import lax
from jax.experimental import pallas as pl
from jax.experimental.pallas import tpu as pltpu
from jax.sharding import PartitionSpec as P

transverse_speed = 0.35
mixing_coefficient = 0.15
supplied_power = 0.5
axial_drift = 64.0

MESH = pl.DeviceIdType.MESH
LANES = 128
RING_Y = 4


def spread(ref, value):
    for a in range(2):
        for b in range(2):
            ref[pl.ds(8 * (2 * a + b), 8), :] = value[8 * a : 8 * a + 8, LANES * b : LANES * (b + 1)]


def gathered(ref):
    parts = [ref[pl.ds(8 * t, 8), :] for t in range(4)]
    return jnp.concatenate(
        [jnp.concatenate(parts[:2], axis=1), jnp.concatenate(parts[2:], axis=1)], axis=0
    )


def kernel(
    axial,
    rows,
    layers,
    first_layer,
    depth,
    warmth_hbm,
    supply_hbm,
    lower_hbm,
    higher_hbm,
    ratio_hbm,
    group_hbm,
    region_hbm,
    sense_hbm,
    out_ref,
    warmth,
    supply,
    lower,
    higher,
    group,
    ratio,
    region,
    sense,
    gain,
    scale,
    low_scale,
    below,
    above,
    unit,
    rhs,
    halo_out,
    halo_low,
    halo_high,
    mat_out,
    mat_in,
    rhs_out,
    rhs_in,
    edge_out,
    edge_in,
    alpha,
    beta,
    load_sem,
    small_sem,
    own_sem,
    send_sem,
    recv_sem,
):
    me = lax.axis_index("axial")
    row = lax.axis_index("row")
    layer_count = axial // RING_Y
    solvers = layers * RING_Y
    g_size = axial // solvers
    my_layer = lax.rem(me // RING_Y - first_layer + layer_count, layer_count)
    my_solver = my_layer * RING_Y + lax.rem(me, RING_Y)
    solving = my_layer < layers
    has_low = row > 0
    has_high = row < rows - 1

    def device_of(s):
        return lax.rem(s // RING_Y + first_layer, layer_count) * RING_Y + lax.rem(s, RING_Y)

    barrier = pltpu.get_barrier_semaphore()

    @pl.when(has_low)
    def _():
        pl.semaphore_signal(barrier, inc=1, device_id=(row - 1, me), device_id_type=MESH)

    @pl.when(has_high)
    def _():
        pl.semaphore_signal(barrier, inc=1, device_id=(row + 1, me), device_id_type=MESH)

    def greet(j, carry):
        @pl.when(j != me)
        def _():
            pl.semaphore_signal(barrier, inc=1, device_id=(row, j), device_id_type=MESH)

        return carry

    def greet_solver(s, carry):
        return greet(device_of(s), carry)

    if layers == layer_count:
        lax.fori_loop(0, axial, greet, 0)
    else:

        @pl.when(solving)
        def _():
            lax.fori_loop(0, axial, greet, 0)

        @pl.when(jnp.logical_not(solving))
        def _():
            lax.fori_loop(0, solvers, greet_solver, 0)

    loads = [
        pltpu.make_async_copy(source, target, load_sem.at[i])
        for i, (source, target) in enumerate(
            [
                (warmth_hbm, warmth),
                (higher_hbm, higher),
                (lower_hbm, lower),
                (supply_hbm, supply),
                (group_hbm, group),
            ]
        )
    ]
    smalls = [
        pltpu.make_async_copy(source, target, small_sem.at[i])
        for i, (source, target) in enumerate(
            [(ratio_hbm, ratio), (region_hbm, region), (sense_hbm, sense)]
        )
    ]
    for copy in loads + smalls:
        copy.start()

    loads[0].wait()
    for z in range(depth):
        halo_out[0, pl.ds(z, 1), :] = warmth[pl.ds(16 * z, 1), :]
        halo_out[1, pl.ds(z, 1), :] = warmth[pl.ds(16 * z + 15, 1), :]

    others = jnp.where(solving, axial - 1, solvers)
    pl.semaphore_wait(barrier, others + has_low.astype(jnp.int32) + has_high.astype(jnp.int32))

    to_low = functools.partial(
        pltpu.make_async_remote_copy,
        halo_out.at[0],
        halo_high,
        send_sem.at[0],
        recv_sem.at[0],
        device_id_type=MESH,
    )
    to_high = functools.partial(
        pltpu.make_async_remote_copy,
        halo_out.at[1],
        halo_low,
        send_sem.at[1],
        recv_sem.at[1],
        device_id_type=MESH,
    )

    @pl.when(has_low)
    def _():
        to_low(device_id=(row - 1, me)).start()

    @pl.when(has_high)
    def _():
        to_high(device_id=(row + 1, me)).start()

    @pl.when(jnp.logical_not(has_low))
    def _():
        halo_low[...] = jnp.zeros_like(halo_low)

    @pl.when(jnp.logical_not(has_high))
    def _():
        halo_high[...] = jnp.zeros_like(halo_high)

    def slab(z):
        return pl.ds(16 * z, 16)

    loads[1].wait()
    loads[2].wait()
    kept = jnp.ones((16, 256), jnp.float32)
    weight = jnp.ones((16, 256), jnp.float32)
    source = jnp.zeros((16, 256), jnp.float32)
    last = depth - 1
    for z in range(last):
        low = lower[slab(z), :] + axial_drift
        high = higher[slab(z), :]
        excess = 1.0 + low * kept
        inverse = 1.0 / (excess + high)
        low_ratio = low * inverse
        gain[slab(z), :] = high * inverse
        scale[slab(z), :] = inverse
        low_scale[slab(z), :] = low_ratio
        kept = excess * inverse
        weight = low_ratio * weight
        source = inverse + low_ratio * source
        below[slab(z), :] = weight
        unit[slab(z), :] = source
    low_last = lower[slab(last), :] + axial_drift
    inverse_high = 1.0 / higher[slab(last), :]
    spread(mat_out.at[0], low_last * weight * inverse_high)
    spread(mat_out.at[1], (1.0 + low_last * source) * inverse_high)
    reach_low = weight
    reach_high = gain[slab(last - 1), :]
    response = source
    above[slab(last - 1), :] = reach_high
    for z in reversed(range(last - 1)):
        factor = gain[slab(z), :]
        reach_high = factor * reach_high
        reach_low = below[slab(z), :] + factor * reach_low
        response = unit[slab(z), :] + factor * response
        above[slab(z), :] = reach_high
        below[slab(z), :] = reach_low
    spread(mat_out.at[2], response)
    spread(mat_out.at[3], reach_high)

    def scatter(out, into, which):
        own = pltpu.make_async_copy(
            out.at[:, pl.ds(my_solver * g_size, g_size)],
            into.at[:, pl.ds(me * g_size, g_size)],
            own_sem.at[which],
        )

        def send(s, carry):
            target = device_of(s)

            @pl.when(target != me)
            def _():
                pltpu.make_async_remote_copy(
                    out.at[:, pl.ds(s * g_size, g_size)],
                    into.at[:, pl.ds(me * g_size, g_size)],
                    send_sem.at[2 + which],
                    recv_sem.at[2 + which],
                    device_id=(row, target),
                    device_id_type=MESH,
                ).start()

            return carry

        lax.fori_loop(0, solvers, send, 0)

        @pl.when(solving)
        def _():
            own.start()

        return own

    def drain(ref, sem, count):
        part = ref.at[:, pl.ds(0, count)]
        pltpu.make_async_copy(part, part, sem).wait()

    own_matrix = scatter(mat_out, mat_in, 0)

    for copy in [loads[3], loads[4]] + smalls:
        copy.wait()
    kind = group[...]
    share = jnp.zeros((16, 256), jnp.float32)
    for c in range(ratio.shape[0]):
        share = jnp.where(kind == c, transverse_speed * ratio[c], share)
    row_at = lax.broadcasted_iota(jnp.int32, (16, 256), 0)
    lane_at = lax.broadcasted_iota(jnp.int32, (16, 256), 1)
    centre = (1.0 - 4.0 * mixing_coefficient) - share
    share_low = jnp.where(row_at == 0, 0.0, share)
    mixing_low = jnp.where(row_at == 0, 0.0, mixing_coefficient)
    share_high = jnp.where(row_at == 15, 0.0, share)
    mixing_high = jnp.where(row_at == 15, 0.0, mixing_coefficient)
    mixing_left = jnp.where(lane_at == 0, 0.0, mixing_coefficient)
    mixing_right = jnp.where(lane_at == 255, 0.0, mixing_coefficient)

    def direction(z):
        return sense[region[z]].astype(jnp.float32)

    for z in range(depth):
        forward = direction(z)
        here = warmth[slab(z), :]
        rhs[slab(z), :] = (
            centre * here
            + (mixing_low + forward * share_low) * pltpu.roll(here, 1, 0)
            + (mixing_high + (1.0 - forward) * share_high) * pltpu.roll(here, 15, 0)
            + mixing_left * pltpu.roll(here, 1, 1)
            + mixing_right * pltpu.roll(here, 255, 1)
            + supplied_power * supply[slab(z), :]
        )

    @pl.when(has_high)
    def _():
        to_low(device_id=(row, me)).wait_recv()

    @pl.when(has_low)
    def _():
        to_high(device_id=(row, me)).wait_recv()

    edge_share_low = share[0:8, :] - share_low[0:8, :]
    edge_mixing_low = mixing_coefficient - mixing_low[0:8, :]
    edge_share_high = share[8:16, :] - share_high[8:16, :]
    edge_mixing_high = mixing_coefficient - mixing_high[8:16, :]

    def whole_rhs(z):
        forward = direction(z)
        low_row = (edge_mixing_low + forward * edge_share_low) * halo_low[pl.ds(z, 1), :]
        high_row = (edge_mixing_high + (1.0 - forward) * edge_share_high) * halo_high[pl.ds(z, 1), :]
        return rhs[slab(z), :] + jnp.concatenate([low_row, high_row], axis=0)

    value = jnp.zeros((16, 256), jnp.float32)
    for z in range(last):
        value = scale[slab(z), :] * whole_rhs(z) + low_scale[slab(z), :] * value
        rhs[slab(z), :] = value
    spread(rhs_out.at[0], (whole_rhs(last) + low_last * value) * inverse_high)
    for z in reversed(range(last - 1)):
        value = rhs[slab(z), :] + gain[slab(z), :] * value
        rhs[slab(z), :] = value
    spread(rhs_out.at[1], value)
    own_rhs = scatter(rhs_out, rhs_in, 1)

    lines = axial * g_size
    own_back = pltpu.make_async_copy(
        edge_out.at[:, pl.ds(me * g_size, g_size)],
        edge_in.at[:, pl.ds(my_solver * g_size, g_size)],
        own_sem.at[2],
    )

    @pl.when(solving)
    def _():
        at = lax.broadcasted_iota(jnp.int32, (lines, LANES), 0)

        def down(x, blocks):
            return pltpu.roll(x, blocks * g_size, 0)

        def up(x, blocks):
            return pltpu.roll(x, lines - blocks * g_size, 0)

        is_first = at < g_size
        is_last = at >= lines - g_size
        drain(mat_in, recv_sem.at[2], (axial - 1) * g_size)
        own_matrix.wait()
        low = mat_in[0]
        excess = mat_in[1] + jnp.where(is_last, 1.0, up(mat_in[2], 1))
        high = jnp.where(is_last, 0.0, up(mat_in[3], 1))
        excess = jnp.where(is_first, excess + low, excess)
        low = jnp.where(is_first, 0.0, low)
        level, stride = 0, 1
        while stride < axial:
            inverse = 1.0 / (low + excess + high)
            a = low * down(inverse, stride)
            b = high * up(inverse, stride)
            alpha[level] = a
            beta[level] = b
            excess = excess + a * down(excess, stride) + b * up(excess, stride)
            low = a * down(low, stride)
            high = b * up(high, stride)
            level, stride = level + 1, stride * 2
        final = 1.0 / excess

        drain(rhs_in, recv_sem.at[3], (axial - 1) * g_size)
        own_rhs.wait()
        r = rhs_in[0] + jnp.where(is_last, 0.0, up(rhs_in[1], 1))
        level, stride = 0, 1
        while stride < axial:
            r = r + alpha[level] * down(r, stride) + beta[level] * up(r, stride)
            level, stride = level + 1, stride * 2
        r = r * final
        edge_out[1] = r
        edge_out[0] = jnp.where(is_first, 0.0, down(r, 1))

        def send(j, carry):
            @pl.when(j != me)
            def _():
                pltpu.make_async_remote_copy(
                    edge_out.at[:, pl.ds(j * g_size, g_size)],
                    edge_in.at[:, pl.ds(my_solver * g_size, g_size)],
                    send_sem.at[4],
                    recv_sem.at[4],
                    device_id=(row, j),
                    device_id_type=MESH,
                ).start()

            return carry

        lax.fori_loop(0, axial, send, 0)
        own_back.start()
        own_back.wait()
        drain(edge_in, recv_sem.at[4], axial - g_size)

    if layers != layer_count:

        @pl.when(jnp.logical_not(solving))
        def _():
            drain(edge_in, recv_sem.at[4], axial)

    below_edge = gathered(edge_in.at[0])
    own_edge = gathered(edge_in.at[1])
    for z in range(last):
        out_ref[slab(z), :] = (
            rhs[slab(z), :] + below[slab(z), :] * below_edge + above[slab(z), :] * own_edge
        )
    out_ref[slab(last), :] = own_edge

    @pl.when(has_low)
    def _():
        to_low(device_id=(row, me)).wait_send()

    @pl.when(has_high)
    def _():
        to_high(device_id=(row, me)).wait_send()

    @pl.when(solving)
    def _():
        drain(mat_out, send_sem.at[2], axial - g_size)
        drain(rhs_out, send_sem.at[3], axial - g_size)
        drain(edge_out, send_sem.at[4], (axial - 1) * g_size)

    if layers != layer_count:

        @pl.when(jnp.logical_not(solving))
        def _():
            drain(mat_out, send_sem.at[2], axial)
            drain(rhs_out, send_sem.at[3], axial)


def solution(mesh):
    axial, rows = mesh.shape["axial"], mesh.shape["row"]
    layer_count = axial // RING_Y
    layers, first_layer = layer_count, 0

    def on_device(warmth, supply, lower, higher, ratio, group, region, sense):
        depth, width, length = warmth.shape
        flat = (depth * width, length)
        lines = axial * (layer_count // layers)
        levels = axial.bit_length() - 1
        field = pltpu.VMEM(flat, jnp.float32)
        halo = pltpu.VMEM((depth, length), jnp.float32)
        out = pl.pallas_call(
            functools.partial(kernel, axial, rows, layers, first_layer, depth),
            out_shape=jax.ShapeDtypeStruct(flat, jnp.float32),
            in_specs=[pl.BlockSpec(memory_space=pl.ANY)] * 8,
            out_specs=pl.BlockSpec(memory_space=pltpu.VMEM),
            scratch_shapes=[
                field,
                field,
                field,
                field,
                pltpu.VMEM(group.shape, jnp.int32),
                pltpu.SMEM(ratio.shape, jnp.float32),
                pltpu.SMEM(region.shape, jnp.int32),
                pltpu.SMEM(sense.shape, jnp.int32),
                field,
                field,
                field,
                field,
                field,
                field,
                field,
                pltpu.VMEM((2, depth, length), jnp.float32),
                halo,
                halo,
                pltpu.VMEM((4, axial, LANES), jnp.float32),
                pltpu.VMEM((4, lines, LANES), jnp.float32),
                pltpu.VMEM((2, axial, LANES), jnp.float32),
                pltpu.VMEM((2, lines, LANES), jnp.float32),
                pltpu.VMEM((2, lines, LANES), jnp.float32),
                pltpu.VMEM((2, axial, LANES), jnp.float32),
                pltpu.VMEM((levels, lines, LANES), jnp.float32),
                pltpu.VMEM((levels, lines, LANES), jnp.float32),
                pltpu.SemaphoreType.DMA((5,)),
                pltpu.SemaphoreType.DMA((3,)),
                pltpu.SemaphoreType.DMA((3,)),
                pltpu.SemaphoreType.DMA((5,)),
                pltpu.SemaphoreType.DMA((5,)),
            ],
            compiler_params=pltpu.CompilerParams(
                collective_id=0, has_side_effects=True, vmem_limit_bytes=32 * 1024 * 1024
            ),
        )(
            warmth.reshape(flat),
            supply.reshape(flat),
            lower.reshape(flat),
            higher.reshape(flat),
            ratio,
            group,
            region,
            sense,
        )
        return out.reshape(warmth.shape)

    placed = (
        P("axial", "row", None),
        P("axial", "row", None),
        P("axial", "row", None),
        P("axial", "row", None),
        P(),
        P("row", None),
        P("axial"),
        P(),
    )
    return jax.shard_map(
        on_device, mesh=mesh, in_specs=placed, out_specs=P("axial", "row", None), check_vma=False
    )
```

```python
import functools

import jax
import jax.numpy as jnp
from jax import lax
from jax.experimental import pallas as pl
from jax.experimental.pallas import tpu as pltpu
from jax.sharding import PartitionSpec as P

transverse_speed = 0.35
mixing_coefficient = 0.15
supplied_power = 0.5
axial_drift = 64.0

MESH = pl.DeviceIdType.MESH
LANES = 128
RING_Y = 4


def spread(ref, value):
    for a in range(2):
        for b in range(2):
            ref[pl.ds(8 * (2 * a + b), 8), :] = value[8 * a : 8 * a + 8, LANES * b : LANES * (b + 1)]


def gathered(ref):
    parts = [ref[pl.ds(8 * t, 8), :] for t in range(4)]
    return jnp.concatenate(
        [jnp.concatenate(parts[:2], axis=1), jnp.concatenate(parts[2:], axis=1)], axis=0
    )


def kernel(
    axial,
    rows,
    layers,
    first_layer,
    depth,
    warmth_hbm,
    supply_hbm,
    lower_hbm,
    higher_hbm,
    ratio_hbm,
    group_hbm,
    region_hbm,
    sense_hbm,
    out_ref,
    warmth,
    supply,
    lower,
    higher,
    group,
    ratio,
    region,
    sense,
    gain,
    scale,
    low_scale,
    below,
    above,
    unit,
    rhs,
    halo_out,
    halo_low,
    halo_high,
    mat_out,
    mat_in,
    rhs_out,
    rhs_in,
    edge_out,
    edge_in,
    alpha,
    beta,
    load_sem,
    small_sem,
    own_sem,
    send_sem,
    recv_sem,
):
    me = lax.axis_index("axial")
    row = lax.axis_index("row")
    layer_count = axial // RING_Y
    solvers = layers * RING_Y
    g_size = axial // solvers
    my_layer = lax.rem(me // RING_Y - first_layer + layer_count, layer_count)
    my_solver = my_layer * RING_Y + lax.rem(me, RING_Y)
    solving = my_layer < layers
    has_low = row > 0
    has_high = row < rows - 1

    def device_of(s):
        return lax.rem(s // RING_Y + first_layer, layer_count) * RING_Y + lax.rem(s, RING_Y)

    barrier = pltpu.get_barrier_semaphore()

    @pl.when(has_low)
    def _():
        pl.semaphore_signal(barrier, inc=1, device_id=(row - 1, me), device_id_type=MESH)

    @pl.when(has_high)
    def _():
        pl.semaphore_signal(barrier, inc=1, device_id=(row + 1, me), device_id_type=MESH)

    def greet(j, carry):
        @pl.when(j != me)
        def _():
            pl.semaphore_signal(barrier, inc=1, device_id=(row, j), device_id_type=MESH)

        return carry

    @pl.when(solving)
    def _():
        lax.fori_loop(0, axial, greet, 0)

    loads = [
        pltpu.make_async_copy(source, target, load_sem.at[i])
        for i, (source, target) in enumerate(
            [
                (warmth_hbm, warmth),
                (higher_hbm, higher),
                (lower_hbm, lower),
                (supply_hbm, supply),
                (group_hbm, group),
            ]
        )
    ]
    smalls = [
        pltpu.make_async_copy(source, target, small_sem.at[i])
        for i, (source, target) in enumerate(
            [(ratio_hbm, ratio), (region_hbm, region), (sense_hbm, sense)]
        )
    ]
    for copy in loads + smalls:
        copy.start()

    loads[0].wait()
    for z in range(depth):
        halo_out[0, pl.ds(z, 1), :] = warmth[pl.ds(16 * z, 1), :]
        halo_out[1, pl.ds(z, 1), :] = warmth[pl.ds(16 * z + 15, 1), :]

    others = jnp.where(solving, solvers - 1, solvers)
    pl.semaphore_wait(barrier, others + has_low.astype(jnp.int32) + has_high.astype(jnp.int32))

    to_low = functools.partial(
        pltpu.make_async_remote_copy,
        halo_out.at[0],
        halo_high,
        send_sem.at[0],
        recv_sem.at[0],
        device_id_type=MESH,
    )
    to_high = functools.partial(
        pltpu.make_async_remote_copy,
        halo_out.at[1],
        halo_low,
        send_sem.at[1],
        recv_sem.at[1],
        device_id_type=MESH,
    )

    @pl.when(has_low)
    def _():
        to_low(device_id=(row - 1, me)).start()

    @pl.when(has_high)
    def _():
        to_high(device_id=(row + 1, me)).start()

    @pl.when(jnp.logical_not(has_low))
    def _():
        halo_low[...] = jnp.zeros_like(halo_low)

    @pl.when(jnp.logical_not(has_high))
    def _():
        halo_high[...] = jnp.zeros_like(halo_high)

    def slab(z):
        return pl.ds(16 * z, 16)

    loads[1].wait()
    loads[2].wait()
    kept = jnp.ones((16, 256), jnp.float32)
    weight = jnp.ones((16, 256), jnp.float32)
    source = jnp.zeros((16, 256), jnp.float32)
    last = depth - 1
    for z in range(last):
        low = lower[slab(z), :] + axial_drift
        high = higher[slab(z), :]
        excess = 1.0 + low * kept
        inverse = 1.0 / (excess + high)
        low_ratio = low * inverse
        gain[slab(z), :] = high * inverse
        scale[slab(z), :] = inverse
        low_scale[slab(z), :] = low_ratio
        kept = excess * inverse
        weight = low_ratio * weight
        source = inverse + low_ratio * source
        below[slab(z), :] = weight
        unit[slab(z), :] = source
    low_last = lower[slab(last), :] + axial_drift
    inverse_high = 1.0 / higher[slab(last), :]
    spread(mat_out.at[0], low_last * weight * inverse_high)
    spread(mat_out.at[1], (1.0 + low_last * source) * inverse_high)
    reach_low = weight
    reach_high = gain[slab(last - 1), :]
    response = source
    above[slab(last - 1), :] = reach_high
    for z in reversed(range(last - 1)):
        factor = gain[slab(z), :]
        reach_high = factor * reach_high
        reach_low = below[slab(z), :] + factor * reach_low
        response = unit[slab(z), :] + factor * response
        above[slab(z), :] = reach_high
        below[slab(z), :] = reach_low
    spread(mat_out.at[2], response)
    spread(mat_out.at[3], reach_high)

    def scatter(out, into, which):
        own = pltpu.make_async_copy(
            out.at[:, pl.ds(my_solver * g_size, g_size)],
            into.at[:, pl.ds(me * g_size, g_size)],
            own_sem.at[which],
        )

        def send(s, carry):
            target = device_of(s)

            @pl.when(target != me)
            def _():
                pltpu.make_async_remote_copy(
                    out.at[:, pl.ds(s * g_size, g_size)],
                    into.at[:, pl.ds(me * g_size, g_size)],
                    send_sem.at[2 + which],
                    recv_sem.at[2 + which],
                    device_id=(row, target),
                    device_id_type=MESH,
                ).start()

            return carry

        lax.fori_loop(0, solvers, send, 0)

        @pl.when(solving)
        def _():
            own.start()

        return own

    def drain(ref, sem, count):
        part = ref.at[:, pl.ds(0, count)]
        pltpu.make_async_copy(part, part, sem).wait()

    own_matrix = scatter(mat_out, mat_in, 0)

    for copy in [loads[3], loads[4]] + smalls:
        copy.wait()
    kind = group[...]
    share = jnp.zeros((16, 256), jnp.float32)
    for c in range(ratio.shape[0]):
        share = jnp.where(kind == c, transverse_speed * ratio[c], share)
    row_at = lax.broadcasted_iota(jnp.int32, (16, 256), 0)
    lane_at = lax.broadcasted_iota(jnp.int32, (16, 256), 1)
    centre = (1.0 - 4.0 * mixing_coefficient) - share
    share_low = jnp.where(row_at == 0, 0.0, share)
    mixing_low = jnp.where(row_at == 0, 0.0, mixing_coefficient)
    share_high = jnp.where(row_at == 15, 0.0, share)
    mixing_high = jnp.where(row_at == 15, 0.0, mixing_coefficient)
    mixing_left = jnp.where(lane_at == 0, 0.0, mixing_coefficient)
    mixing_right = jnp.where(lane_at == 255, 0.0, mixing_coefficient)

    def direction(z):
        return sense[region[z]].astype(jnp.float32)

    for z in range(depth):
        forward = direction(z)
        here = warmth[slab(z), :]
        rhs[slab(z), :] = (
            centre * here
            + (mixing_low + forward * share_low) * pltpu.roll(here, 1, 0)
            + (mixing_high + (1.0 - forward) * share_high) * pltpu.roll(here, 15, 0)
            + mixing_left * pltpu.roll(here, 1, 1)
            + mixing_right * pltpu.roll(here, 255, 1)
            + supplied_power * supply[slab(z), :]
        )

    @pl.when(has_high)
    def _():
        to_low(device_id=(row, me)).wait_recv()

    @pl.when(has_low)
    def _():
        to_high(device_id=(row, me)).wait_recv()

    edge_share_low = share[0:8, :] - share_low[0:8, :]
    edge_mixing_low = mixing_coefficient - mixing_low[0:8, :]
    edge_share_high = share[8:16, :] - share_high[8:16, :]
    edge_mixing_high = mixing_coefficient - mixing_high[8:16, :]

    def whole_rhs(z):
        forward = direction(z)
        low_row = (edge_mixing_low + forward * edge_share_low) * halo_low[pl.ds(z, 1), :]
        high_row = (edge_mixing_high + (1.0 - forward) * edge_share_high) * halo_high[pl.ds(z, 1), :]
        return rhs[slab(z), :] + jnp.concatenate([low_row, high_row], axis=0)

    value = jnp.zeros((16, 256), jnp.float32)
    for z in range(last):
        value = scale[slab(z), :] * whole_rhs(z) + low_scale[slab(z), :] * value
        rhs[slab(z), :] = value
    spread(rhs_out.at[0], (whole_rhs(last) + low_last * value) * inverse_high)
    for z in reversed(range(last - 1)):
        value = rhs[slab(z), :] + gain[slab(z), :] * value
        rhs[slab(z), :] = value
    spread(rhs_out.at[1], value)
    own_rhs = scatter(rhs_out, rhs_in, 1)

    lines = axial * g_size
    own_back = pltpu.make_async_copy(
        edge_out.at[:, pl.ds(me * g_size, g_size)],
        edge_in.at[:, pl.ds(my_solver * g_size, g_size)],
        own_sem.at[2],
    )

    @pl.when(solving)
    def _():
        at = lax.broadcasted_iota(jnp.int32, (lines, LANES), 0)

        def down(x, blocks):
            return pltpu.roll(x, blocks * g_size, 0)

        def up(x, blocks):
            return pltpu.roll(x, lines - blocks * g_size, 0)

        is_first = at < g_size
        is_last = at >= lines - g_size
        drain(mat_in, recv_sem.at[2], (axial - 1) * g_size)
        own_matrix.wait()
        low = mat_in[0]
        excess = mat_in[1] + jnp.where(is_last, 1.0, up(mat_in[2], 1))
        high = jnp.where(is_last, 0.0, up(mat_in[3], 1))
        excess = jnp.where(is_first, excess + low, excess)
        low = jnp.where(is_first, 0.0, low)
        level, stride = 0, 1
        while stride < axial:
            inverse = 1.0 / (low + excess + high)
            a = low * down(inverse, stride)
            b = high * up(inverse, stride)
            alpha[level] = a
            beta[level] = b
            excess = excess + a * down(excess, stride) + b * up(excess, stride)
            low = a * down(low, stride)
            high = b * up(high, stride)
            level, stride = level + 1, stride * 2
        final = 1.0 / excess

        drain(rhs_in, recv_sem.at[3], (axial - 1) * g_size)
        own_rhs.wait()
        r = rhs_in[0] + jnp.where(is_last, 0.0, up(rhs_in[1], 1))
        level, stride = 0, 1
        while stride < axial:
            r = r + alpha[level] * down(r, stride) + beta[level] * up(r, stride)
            level, stride = level + 1, stride * 2
        r = r * final
        edge_out[1] = r
        edge_out[0] = jnp.where(is_first, 0.0, down(r, 1))

        def send(j, carry):
            @pl.when(j != me)
            def _():
                pltpu.make_async_remote_copy(
                    edge_out.at[:, pl.ds(j * g_size, g_size)],
                    edge_in.at[:, pl.ds(my_solver * g_size, g_size)],
                    send_sem.at[4],
                    recv_sem.at[4],
                    device_id=(row, j),
                    device_id_type=MESH,
                ).start()

            return carry

        lax.fori_loop(0, axial, send, 0)
        own_back.start()
        own_back.wait()
        drain(edge_in, recv_sem.at[4], axial - g_size)

    if layers != layer_count:

        @pl.when(jnp.logical_not(solving))
        def _():
            drain(edge_in, recv_sem.at[4], axial)

    below_edge = gathered(edge_in.at[0])
    own_edge = gathered(edge_in.at[1])
    for z in range(last):
        out_ref[slab(z), :] = (
            rhs[slab(z), :] + below[slab(z), :] * below_edge + above[slab(z), :] * own_edge
        )
    out_ref[slab(last), :] = own_edge

    @pl.when(has_low)
    def _():
        to_low(device_id=(row, me)).wait_send()

    @pl.when(has_high)
    def _():
        to_high(device_id=(row, me)).wait_send()

    @pl.when(solving)
    def _():
        drain(mat_out, send_sem.at[2], axial - g_size)
        drain(rhs_out, send_sem.at[3], axial - g_size)
        drain(edge_out, send_sem.at[4], (axial - 1) * g_size)

    if layers != layer_count:

        @pl.when(jnp.logical_not(solving))
        def _():
            drain(mat_out, send_sem.at[2], axial)
            drain(rhs_out, send_sem.at[3], axial)


def solution(mesh):
    axial, rows = mesh.shape["axial"], mesh.shape["row"]
    layer_count = axial // RING_Y
    layers, first_layer = 2, 0

    def on_device(warmth, supply, lower, higher, ratio, group, region, sense):
        depth, width, length = warmth.shape
        flat = (depth * width, length)
        lines = axial * (layer_count // layers)
        levels = axial.bit_length() - 1
        field = pltpu.VMEM(flat, jnp.float32)
        halo = pltpu.VMEM((depth, length), jnp.float32)
        out = pl.pallas_call(
            functools.partial(kernel, axial, rows, layers, first_layer, depth),
            out_shape=jax.ShapeDtypeStruct(flat, jnp.float32),
            in_specs=[pl.BlockSpec(memory_space=pltpu.HBM)] * 8,
            out_specs=pl.BlockSpec(memory_space=pltpu.VMEM),
            scratch_shapes=[
                field,
                field,
                field,
                field,
                pltpu.VMEM(group.shape, jnp.int32),
                pltpu.SMEM(ratio.shape, jnp.float32),
                pltpu.SMEM(region.shape, jnp.int32),
                pltpu.SMEM(sense.shape, jnp.int32),
                field,
                field,
                field,
                field,
                field,
                field,
                field,
                pltpu.VMEM((2, depth, length), jnp.float32),
                halo,
                halo,
                pltpu.VMEM((4, axial, LANES), jnp.float32),
                pltpu.VMEM((4, lines, LANES), jnp.float32),
                pltpu.VMEM((2, axial, LANES), jnp.float32),
                pltpu.VMEM((2, lines, LANES), jnp.float32),
                pltpu.VMEM((2, lines, LANES), jnp.float32),
                pltpu.VMEM((2, axial, LANES), jnp.float32),
                pltpu.VMEM((levels, lines, LANES), jnp.float32),
                pltpu.VMEM((levels, lines, LANES), jnp.float32),
                pltpu.SemaphoreType.DMA((5,)),
                pltpu.SemaphoreType.DMA((3,)),
                pltpu.SemaphoreType.DMA((3,)),
                pltpu.SemaphoreType.DMA((5,)),
                pltpu.SemaphoreType.DMA((5,)),
            ],
            compiler_params=pltpu.CompilerParams(
                collective_id=0, has_side_effects=True, vmem_limit_bytes=32 * 1024 * 1024
            ),
        )(
            *(
                pltpu.with_memory_space_constraint(x, pltpu.HBM)
                for x in (
                    warmth.reshape(flat),
                    supply.reshape(flat),
                    lower.reshape(flat),
                    higher.reshape(flat),
                    ratio,
                    group,
                    region,
                    sense,
                )
            )
        )
        return out.reshape(warmth.shape)

    placed = (
        P("axial", "row", None),
        P("axial", "row", None),
        P("axial", "row", None),
        P("axial", "row", None),
        P(),
        P("row", None),
        P("axial"),
        P(),
    )
    return jax.shard_map(
        on_device, mesh=mesh, in_specs=placed, out_specs=P("axial", "row", None), check_vma=False
    )
```

```python
import functools

import jax
import jax.numpy as jnp
from jax import lax
from jax.experimental import pallas as pl
from jax.experimental.pallas import tpu as pltpu
from jax.sharding import PartitionSpec as P

transverse_speed = 0.35
mixing_coefficient = 0.15
supplied_power = 0.5
axial_drift = 64.0

MESH = pl.DeviceIdType.MESH
LANES = 128
RING_Y = 4
LAYERS = 2


def spread(ref, value):
    for a in range(2):
        for b in range(2):
            ref[pl.ds(8 * (2 * a + b), 8), :] = value[8 * a : 8 * a + 8, LANES * b : LANES * (b + 1)]


def gathered(ref):
    parts = [ref[pl.ds(8 * t, 8), :] for t in range(4)]
    return jnp.concatenate(
        [jnp.concatenate(parts[:2], axis=1), jnp.concatenate(parts[2:], axis=1)], axis=0
    )


def kernel(
    axial,
    rows,
    first_layer,
    depth,
    warmth_hbm,
    supply_hbm,
    lower_hbm,
    higher_hbm,
    ratio_hbm,
    group_hbm,
    region_hbm,
    sense_hbm,
    out_ref,
    warmth,
    supply,
    lower,
    higher,
    group,
    ratio,
    region,
    sense,
    gain,
    scale,
    low_scale,
    below,
    above,
    unit,
    rhs,
    part,
    halo_out,
    halo_low,
    halo_high,
    mat_out,
    mat_in,
    rhs_out,
    rhs_in,
    edge_out,
    edge_in,
    side_rhs_out,
    side_rhs_in,
    side_edge_out,
    side_edge_in,
    alpha,
    beta,
    side_alpha,
    side_beta,
    finals,
    load_sem,
    small_sem,
    own_sem,
    send_sem,
    recv_sem,
):
    me = lax.axis_index("axial")
    row = lax.axis_index("row")
    layer_count = axial // RING_Y
    solvers = LAYERS * RING_Y
    g_size = axial // solvers
    my_y = lax.rem(me, RING_Y)
    my_layer = lax.rem(me // RING_Y - first_layer + layer_count, layer_count)
    my_solver = 2 * my_y + lax.rem(my_layer + my_y // 2, 2)
    solving = my_layer < LAYERS
    siding = my_layer == 0
    has_low = row > 0
    has_high = row < rows - 1

    def device_of(s):
        layer = lax.rem(s + s // 4, 2)
        return lax.rem(layer + first_layer, layer_count) * RING_Y + s // 2

    def side_device(h):
        return first_layer * RING_Y + h

    barrier = pltpu.get_barrier_semaphore()

    @pl.when(has_low)
    def _():
        pl.semaphore_signal(barrier, inc=1, device_id=(row - 1, me), device_id_type=MESH)

    @pl.when(has_high)
    def _():
        pl.semaphore_signal(barrier, inc=1, device_id=(row + 1, me), device_id_type=MESH)

    def greet(j, carry):
        @pl.when(j != me)
        def _():
            pl.semaphore_signal(barrier, inc=1, device_id=(row, j), device_id_type=MESH)

        return carry

    @pl.when(solving)
    def _():
        lax.fori_loop(0, axial, lambda i, c: greet(axial - 1 - i, c), 0)

    loads = [
        pltpu.make_async_copy(source, target, load_sem.at[i])
        for i, (source, target) in enumerate(
            [
                (higher_hbm, higher),
                (lower_hbm, lower),
                (warmth_hbm, warmth),
                (supply_hbm, supply),
                (group_hbm, group),
            ]
        )
    ]
    smalls = [
        pltpu.make_async_copy(source, target, small_sem.at[i])
        for i, (source, target) in enumerate(
            [(ratio_hbm, ratio), (region_hbm, region), (sense_hbm, sense)]
        )
    ]
    for copy in loads + smalls:
        copy.start()

    def slab(z):
        return pl.ds(16 * z, 16)

    loads[0].wait()
    loads[1].wait()
    kept = jnp.ones((16, 256), jnp.float32)
    weight = jnp.ones((16, 256), jnp.float32)
    source = jnp.zeros((16, 256), jnp.float32)
    last = depth - 1
    for z in range(last):
        low = lower[slab(z), :] + axial_drift
        high = higher[slab(z), :]
        excess = 1.0 + low * kept
        inverse = 1.0 / (excess + high)
        low_ratio = low * inverse
        gain[slab(z), :] = high * inverse
        scale[slab(z), :] = inverse
        low_scale[slab(z), :] = low_ratio
        kept = excess * inverse
        weight = low_ratio * weight
        source = inverse + low_ratio * source
        below[slab(z), :] = weight
        unit[slab(z), :] = source
    low_last = lower[slab(last), :] + axial_drift
    inverse_high = 1.0 / higher[slab(last), :]
    spread(mat_out.at[0], low_last * weight * inverse_high)
    spread(mat_out.at[1], (1.0 + low_last * source) * inverse_high)
    reach_low = weight
    reach_high = gain[slab(last - 1), :]
    response = source
    above[slab(last - 1), :] = reach_high
    for z in reversed(range(last - 1)):
        factor = gain[slab(z), :]
        reach_high = factor * reach_high
        reach_low = below[slab(z), :] + factor * reach_low
        response = unit[slab(z), :] + factor * response
        above[slab(z), :] = reach_high
        below[slab(z), :] = reach_low
    spread(mat_out.at[2], response)
    spread(mat_out.at[3], reach_high)

    loads[2].wait()
    for z in range(depth):
        halo_out[0, pl.ds(z, 1), :] = warmth[pl.ds(16 * z, 1), :]
        halo_out[1, pl.ds(z, 1), :] = warmth[pl.ds(16 * z + 15, 1), :]

    others = jnp.where(solving, solvers - 1, solvers)
    pl.semaphore_wait(barrier, others + has_low.astype(jnp.int32) + has_high.astype(jnp.int32))

    to_low = functools.partial(
        pltpu.make_async_remote_copy,
        halo_out.at[0],
        halo_high,
        send_sem.at[0],
        recv_sem.at[0],
        device_id_type=MESH,
    )
    to_high = functools.partial(
        pltpu.make_async_remote_copy,
        halo_out.at[1],
        halo_low,
        send_sem.at[1],
        recv_sem.at[1],
        device_id_type=MESH,
    )

    @pl.when(has_low)
    def _():
        to_low(device_id=(row - 1, me)).start()

    @pl.when(has_high)
    def _():
        to_high(device_id=(row + 1, me)).start()

    @pl.when(jnp.logical_not(has_low))
    def _():
        halo_low[...] = jnp.zeros_like(halo_low)

    @pl.when(jnp.logical_not(has_high))
    def _():
        halo_high[...] = jnp.zeros_like(halo_high)

    def scatter(out, into, which):
        own = pltpu.make_async_copy(
            out.at[:, pl.ds(my_solver * g_size, g_size)],
            into.at[:, pl.ds(me * g_size, g_size)],
            own_sem.at[which],
        )

        def send(s, carry):
            target = device_of(s)

            @pl.when(target != me)
            def _():
                pltpu.make_async_remote_copy(
                    out.at[:, pl.ds(s * g_size, g_size)],
                    into.at[:, pl.ds(me * g_size, g_size)],
                    send_sem.at[2 + which],
                    recv_sem.at[2 + which],
                    device_id=(row, target),
                    device_id_type=MESH,
                ).start()

            return carry

        lax.fori_loop(0, solvers, send, 0)

        @pl.when(solving)
        def _():
            own.start()

        return own

    def drain(ref, sem, count):
        part = ref.at[:, pl.ds(0, count)]
        pltpu.make_async_copy(part, part, sem).wait()

    own_matrix = scatter(mat_out, mat_in, 0)

    for copy in [loads[3], loads[4]] + smalls:
        copy.wait()
    kind = group[...]
    share = jnp.zeros((16, 256), jnp.float32)
    for c in range(ratio.shape[0]):
        share = jnp.where(kind == c, transverse_speed * ratio[c], share)
    row_at = lax.broadcasted_iota(jnp.int32, (16, 256), 0)
    lane_at = lax.broadcasted_iota(jnp.int32, (16, 256), 1)
    centre = (1.0 - 4.0 * mixing_coefficient) - share
    share_low = jnp.where(row_at == 0, 0.0, share)
    mixing_low = jnp.where(row_at == 0, 0.0, mixing_coefficient)
    share_high = jnp.where(row_at == 15, 0.0, share)
    mixing_high = jnp.where(row_at == 15, 0.0, mixing_coefficient)
    mixing_left = jnp.where(lane_at == 0, 0.0, mixing_coefficient)
    mixing_right = jnp.where(lane_at == 255, 0.0, mixing_coefficient)

    def direction(z):
        return sense[region[z]].astype(jnp.float32)

    for z in range(depth):
        forward = direction(z)
        here = warmth[slab(z), :]
        rhs[slab(z), :] = (
            centre * here
            + (mixing_low + forward * share_low) * pltpu.roll(here, 1, 0)
            + (mixing_high + (1.0 - forward) * share_high) * pltpu.roll(here, 15, 0)
            + mixing_left * pltpu.roll(here, 1, 1)
            + mixing_right * pltpu.roll(here, 255, 1)
            + supplied_power * supply[slab(z), :]
        )

    first_value = scale[slab(0), :] * rhs[slab(0), :]
    value = first_value
    for z in range(1, last):
        value = scale[slab(z), :] * rhs[slab(z), :] + low_scale[slab(z), :] * value
        part[slab(z), :] = value
    spread(rhs_out.at[0], (rhs[slab(last), :] + low_last * value) * inverse_high)
    for z in reversed(range(1, last - 1)):
        value = part[slab(z), :] + gain[slab(z), :] * value
    spread(rhs_out.at[1], first_value + gain[slab(0), :] * value)
    own_rhs = scatter(rhs_out, rhs_in, 1)

    @pl.when(has_high)
    def _():
        to_low(device_id=(row, me)).wait_recv()

    @pl.when(has_low)
    def _():
        to_high(device_id=(row, me)).wait_recv()

    edge_share_low = share[0:8, :] - share_low[0:8, :]
    edge_mixing_low = mixing_coefficient - mixing_low[0:8, :]
    edge_share_high = share[8:16, :] - share_high[8:16, :]
    edge_mixing_high = mixing_coefficient - mixing_high[8:16, :]

    def whole_rhs(z):
        forward = direction(z)
        low_row = (edge_mixing_low + forward * edge_share_low) * halo_low[pl.ds(z, 1), :]
        high_row = (edge_mixing_high + (1.0 - forward) * edge_share_high) * halo_high[pl.ds(z, 1), :]
        return rhs[slab(z), :] + jnp.concatenate([low_row, high_row], axis=0)

    def sides(ref, value):
        for h in range(4):
            x, half = 15 * (h // 2), LANES * (h % 2)
            ref[pl.ds(h, 1), :] = value[x : x + 1, half : half + LANES]

    value = jnp.zeros((16, 256), jnp.float32)
    for z in range(last):
        value = scale[slab(z), :] * whole_rhs(z) + low_scale[slab(z), :] * value
        rhs[slab(z), :] = value
    sides(side_rhs_out.at[0], (whole_rhs(last) + low_last * value) * inverse_high)
    for z in reversed(range(last - 1)):
        value = rhs[slab(z), :] + gain[slab(z), :] * value
        rhs[slab(z), :] = value
    sides(side_rhs_out.at[1], value)
    own_side = pltpu.make_async_copy(
        side_rhs_out.at[:, pl.ds(my_y, 1)], side_rhs_in.at[:, pl.ds(me, 1)], own_sem.at[3]
    )

    def send_side(h, carry):
        target = side_device(h)

        @pl.when(target != me)
        def _():
            pltpu.make_async_remote_copy(
                side_rhs_out.at[:, pl.ds(h, 1)],
                side_rhs_in.at[:, pl.ds(me, 1)],
                send_sem.at[5],
                recv_sem.at[5],
                device_id=(row, target),
                device_id_type=MESH,
            ).start()

        return carry

    lax.fori_loop(0, RING_Y, send_side, 0)

    @pl.when(siding)
    def _():
        own_side.start()

    lines = axial * g_size
    def send_back(j, carry):
        @pl.when(j != me)
        def _():
            pltpu.make_async_remote_copy(
                edge_out.at[:, pl.ds(j * g_size, g_size)],
                edge_in.at[:, pl.ds(my_solver * g_size, g_size)],
                send_sem.at[4],
                recv_sem.at[4],
                device_id=(row, j),
                device_id_type=MESH,
            ).start()

        return carry

    own_back = pltpu.make_async_copy(
        edge_out.at[:, pl.ds(me * g_size, g_size)],
        edge_in.at[:, pl.ds(my_solver * g_size, g_size)],
        own_sem.at[2],
    )

    @pl.when(solving)
    def _():
        at = lax.broadcasted_iota(jnp.int32, (lines, LANES), 0)

        def down(x, blocks):
            return pltpu.roll(x, blocks * g_size, 0)

        def up(x, blocks):
            return pltpu.roll(x, lines - blocks * g_size, 0)

        is_first = at < g_size
        is_last = at >= lines - g_size
        drain(mat_in, recv_sem.at[2], (axial - 1) * g_size)
        own_matrix.wait()
        low = mat_in[0]
        excess = mat_in[1] + jnp.where(is_last, 1.0, up(mat_in[2], 1))
        high = jnp.where(is_last, 0.0, up(mat_in[3], 1))
        excess = jnp.where(is_first, excess + low, excess)
        low = jnp.where(is_first, 0.0, low)
        level, stride = 0, 1
        while stride < axial:
            inverse = 1.0 / (low + excess + high)
            a = low * down(inverse, stride)
            b = high * up(inverse, stride)
            alpha[level] = a
            beta[level] = b
            excess = excess + a * down(excess, stride) + b * up(excess, stride)
            low = a * down(low, stride)
            high = b * up(high, stride)
            level, stride = level + 1, stride * 2
        final = 1.0 / excess
        finals[...] = final

        drain(rhs_in, recv_sem.at[3], (axial - 1) * g_size)
        own_rhs.wait()
        r = rhs_in[0] + jnp.where(is_last, 0.0, up(rhs_in[1], 1))
        level, stride = 0, 1
        while stride < axial:
            r = r + alpha[level] * down(r, stride) + beta[level] * up(r, stride)
            level, stride = level + 1, stride * 2
        r = r * final
        edge_out[1] = r
        edge_out[0] = jnp.where(is_first, 0.0, down(r, 1))

        lax.fori_loop(0, 4, send_back, 0)
        own_back.start()

    own_side_back = pltpu.make_async_copy(
        side_edge_out.at[:, pl.ds(me, 1)], side_edge_in.at[:, pl.ds(my_y, 1)], own_sem.at[4]
    )

    @pl.when(siding)
    def _():
        at = lax.broadcasted_iota(jnp.int32, (axial, LANES), 0)

        def down(x, blocks):
            return pltpu.roll(x, blocks, 0)

        def up(x, blocks):
            return pltpu.roll(x, axial - blocks, 0)

        local = 3 * (my_y // 2)
        levels = alpha.shape[0]
        for level in range(levels):
            side_alpha[level] = alpha[level, pl.ds(local, axial, stride=g_size), :]
            side_beta[level] = beta[level, pl.ds(local, axial, stride=g_size), :]
        final = finals[pl.ds(local, axial, stride=g_size), :]
        drain(side_rhs_in, recv_sem.at[5], axial - 1)
        own_side.wait()
        r = side_rhs_in[0] + jnp.where(at == axial - 1, 0.0, up(side_rhs_in[1], 1))
        level, stride = 0, 1
        while stride < axial:
            r = r + side_alpha[level] * down(r, stride) + side_beta[level] * up(r, stride)
            level, stride = level + 1, stride * 2
        r = r * final
        side_edge_out[1] = r
        side_edge_out[0] = jnp.where(at == 0, 0.0, down(r, 1))

        def send(j, carry):
            @pl.when(j != me)
            def _():
                pltpu.make_async_remote_copy(
                    side_edge_out.at[:, pl.ds(j, 1)],
                    side_edge_in.at[:, pl.ds(my_y, 1)],
                    send_sem.at[6],
                    recv_sem.at[6],
                    device_id=(row, j),
                    device_id_type=MESH,
                ).start()

            return carry

        lax.fori_loop(0, axial, send, 0)
        own_side_back.start()

    @pl.when(solving)
    def _():
        lax.fori_loop(4, axial, send_back, 0)

    @pl.when(siding)
    def _():
        own_side_back.wait()
        drain(side_edge_in, recv_sem.at[6], RING_Y - 1)

    @pl.when(jnp.logical_not(siding))
    def _():
        drain(side_edge_in, recv_sem.at[6], RING_Y)

    @pl.when(solving)
    def _():
        own_back.wait()
        drain(edge_in, recv_sem.at[4], axial - g_size)

    @pl.when(jnp.logical_not(solving))
    def _():
        drain(edge_in, recv_sem.at[4], axial)

    for k in range(2):
        for h, g in enumerate((0, 8, 23, 31)):
            edge_in[k, pl.ds(g, 1), :] = side_edge_in[k, pl.ds(h, 1), :]

    below_edge = gathered(edge_in.at[0])
    own_edge = gathered(edge_in.at[1])
    for z in range(last):
        out_ref[slab(z), :] = (
            rhs[slab(z), :] + below[slab(z), :] * below_edge + above[slab(z), :] * own_edge
        )
    out_ref[slab(last), :] = own_edge

    @pl.when(has_low)
    def _():
        to_low(device_id=(row, me)).wait_send()

    @pl.when(has_high)
    def _():
        to_high(device_id=(row, me)).wait_send()

    @pl.when(solving)
    def _():
        drain(mat_out, send_sem.at[2], axial - g_size)
        drain(rhs_out, send_sem.at[3], axial - g_size)
        drain(edge_out, send_sem.at[4], (axial - 1) * g_size)

    @pl.when(jnp.logical_not(solving))
    def _():
        drain(mat_out, send_sem.at[2], axial)
        drain(rhs_out, send_sem.at[3], axial)

    @pl.when(siding)
    def _():
        drain(side_rhs_out, send_sem.at[5], RING_Y - 1)
        drain(side_edge_out, send_sem.at[6], axial - 1)

    @pl.when(jnp.logical_not(siding))
    def _():
        drain(side_rhs_out, send_sem.at[5], RING_Y)


def solution(mesh):
    axial, rows = mesh.shape["axial"], mesh.shape["row"]
    layer_count = axial // RING_Y
    first_layer = 1

    def on_device(warmth, supply, lower, higher, ratio, group, region, sense):
        depth, width, length = warmth.shape
        flat = (depth * width, length)
        lines = axial * (layer_count // LAYERS)
        levels = axial.bit_length() - 1
        field = pltpu.VMEM(flat, jnp.float32)
        halo = pltpu.VMEM((depth, length), jnp.float32)
        out = pl.pallas_call(
            functools.partial(kernel, axial, rows, first_layer, depth),
            out_shape=jax.ShapeDtypeStruct(flat, jnp.float32),
            in_specs=[pl.BlockSpec(memory_space=pltpu.HBM)] * 8,
            out_specs=pl.BlockSpec(memory_space=pltpu.VMEM),
            scratch_shapes=[
                field,
                field,
                field,
                field,
                pltpu.VMEM(group.shape, jnp.int32),
                pltpu.SMEM(ratio.shape, jnp.float32),
                pltpu.SMEM(region.shape, jnp.int32),
                pltpu.SMEM(sense.shape, jnp.int32),
                field,
                field,
                field,
                field,
                field,
                field,
                field,
                field,
                pltpu.VMEM((2, depth, length), jnp.float32),
                halo,
                halo,
                pltpu.VMEM((4, axial, LANES), jnp.float32),
                pltpu.VMEM((4, lines, LANES), jnp.float32),
                pltpu.VMEM((2, axial, LANES), jnp.float32),
                pltpu.VMEM((2, lines, LANES), jnp.float32),
                pltpu.VMEM((2, lines, LANES), jnp.float32),
                pltpu.VMEM((2, axial, LANES), jnp.float32),
                pltpu.VMEM((2, RING_Y, LANES), jnp.float32),
                pltpu.VMEM((2, axial, LANES), jnp.float32),
                pltpu.VMEM((2, axial, LANES), jnp.float32),
                pltpu.VMEM((2, RING_Y, LANES), jnp.float32),
                pltpu.VMEM((levels, lines, LANES), jnp.float32),
                pltpu.VMEM((levels, lines, LANES), jnp.float32),
                pltpu.VMEM((levels, axial, LANES), jnp.float32),
                pltpu.VMEM((levels, axial, LANES), jnp.float32),
                pltpu.VMEM((lines, LANES), jnp.float32),
                pltpu.SemaphoreType.DMA((5,)),
                pltpu.SemaphoreType.DMA((3,)),
                pltpu.SemaphoreType.DMA((5,)),
                pltpu.SemaphoreType.DMA((7,)),
                pltpu.SemaphoreType.DMA((7,)),
            ],
            compiler_params=pltpu.CompilerParams(
                collective_id=0, has_side_effects=True, vmem_limit_bytes=32 * 1024 * 1024
            ),
        )(
            *(
                pltpu.with_memory_space_constraint(x, pltpu.HBM)
                for x in (
                    warmth.reshape(flat),
                    supply.reshape(flat),
                    lower.reshape(flat),
                    higher.reshape(flat),
                    ratio,
                    group,
                    region,
                    sense,
                )
            )
        )
        return out.reshape(warmth.shape)

    placed = (
        P("axial", "row", None),
        P("axial", "row", None),
        P("axial", "row", None),
        P("axial", "row", None),
        P(),
        P("row", None),
        P("axial"),
        P(),
    )
    return jax.shard_map(
        on_device, mesh=mesh, in_specs=placed, out_specs=P("axial", "row", None), check_vma=False
    )
```

```python
import functools

import jax
import jax.numpy as jnp
from jax import lax
from jax.experimental import pallas as pl
from jax.experimental.pallas import tpu as pltpu
from jax.sharding import PartitionSpec as P

transverse_speed = 0.35
mixing_coefficient = 0.15
supplied_power = 0.5
axial_drift = 64.0

MESH = pl.DeviceIdType.MESH
LANES = 128
RING_Y = 4
PLACES = (0, 8, 1, 9, 12, 4, 13, 5)
BESIDE = (0, 8, 23, 31)
SIDES = (0, 2, 5, 7)


def spread(ref, value):
    for a in range(2):
        for b in range(2):
            ref[pl.ds(8 * (2 * a + b), 8), :] = value[8 * a : 8 * a + 8, LANES * b : LANES * (b + 1)]


def gathered(ref):
    parts = [ref[pl.ds(8 * t, 8), :] for t in range(4)]
    return jnp.concatenate(
        [jnp.concatenate(parts[:2], axis=1), jnp.concatenate(parts[2:], axis=1)], axis=0
    )


def kernel(
    axial,
    rows,
    depth,
    warmth_hbm,
    supply_hbm,
    lower_hbm,
    higher_hbm,
    ratio_hbm,
    group_hbm,
    region_hbm,
    sense_hbm,
    out_ref,
    warmth,
    supply,
    lower,
    higher,
    group,
    ratio,
    region,
    sense,
    gain,
    scale,
    low_scale,
    below,
    above,
    unit,
    rhs,
    part,
    halo_out,
    halo_low,
    halo_high,
    mat_out,
    mat_in,
    rhs_out,
    rhs_in,
    edge_out,
    edge_in,
    side_rhs_out,
    side_rhs_in,
    side_edge_out,
    side_edge_in,
    alpha,
    beta,
    side_alpha,
    side_beta,
    finals,
    load_sem,
    small_sem,
    own_sem,
    send_sem,
    recv_sem,
):
    me = lax.axis_index("axial")
    row = lax.axis_index("row")
    solvers = len(PLACES)
    g_size = axial // solvers
    my_solver = sum((me == place).astype(jnp.int32) * s for s, place in enumerate(PLACES))
    solving = sum((me == place).astype(jnp.int32) for place in PLACES) > 0
    my_side = sum((me == PLACES[s]).astype(jnp.int32) * h for h, s in enumerate(SIDES))
    siding = sum((me == PLACES[s]).astype(jnp.int32) for s in SIDES) > 0
    has_low = row > 0
    has_high = row < rows - 1

    barrier = pltpu.get_barrier_semaphore()

    @pl.when(has_low)
    def _():
        pl.semaphore_signal(barrier, inc=1, device_id=(row - 1, me), device_id_type=MESH)

    @pl.when(has_high)
    def _():
        pl.semaphore_signal(barrier, inc=1, device_id=(row + 1, me), device_id_type=MESH)

    def greet(j, carry):
        @pl.when(j != me)
        def _():
            pl.semaphore_signal(barrier, inc=1, device_id=(row, j), device_id_type=MESH)

        return carry

    @pl.when(solving)
    def _():
        lax.fori_loop(0, axial, lambda i, c: greet(axial - 1 - i, c), 0)

    loads = [
        pltpu.make_async_copy(source, target, load_sem.at[i])
        for i, (source, target) in enumerate(
            [
                (higher_hbm, higher),
                (lower_hbm, lower),
                (warmth_hbm, warmth),
                (supply_hbm, supply),
                (group_hbm, group),
            ]
        )
    ]
    smalls = [
        pltpu.make_async_copy(source, target, small_sem.at[i])
        for i, (source, target) in enumerate(
            [(ratio_hbm, ratio), (region_hbm, region), (sense_hbm, sense)]
        )
    ]
    for copy in loads + smalls:
        copy.start()

    def slab(z):
        return pl.ds(16 * z, 16)

    loads[0].wait()
    loads[1].wait()
    kept = jnp.ones((16, 256), jnp.float32)
    weight = jnp.ones((16, 256), jnp.float32)
    source = jnp.zeros((16, 256), jnp.float32)
    last = depth - 1
    for z in range(last):
        low = lower[slab(z), :] + axial_drift
        high = higher[slab(z), :]
        excess = 1.0 + low * kept
        inverse = 1.0 / (excess + high)
        low_ratio = low * inverse
        gain[slab(z), :] = high * inverse
        scale[slab(z), :] = inverse
        low_scale[slab(z), :] = low_ratio
        kept = excess * inverse
        weight = low_ratio * weight
        source = inverse + low_ratio * source
        below[slab(z), :] = weight
        unit[slab(z), :] = source
    low_last = lower[slab(last), :] + axial_drift
    inverse_high = 1.0 / higher[slab(last), :]
    spread(mat_out.at[0], low_last * weight * inverse_high)
    spread(mat_out.at[1], (1.0 + low_last * source) * inverse_high)
    reach_low = weight
    reach_high = gain[slab(last - 1), :]
    response = source
    above[slab(last - 1), :] = reach_high
    for z in reversed(range(last - 1)):
        factor = gain[slab(z), :]
        reach_high = factor * reach_high
        reach_low = below[slab(z), :] + factor * reach_low
        response = unit[slab(z), :] + factor * response
        above[slab(z), :] = reach_high
        below[slab(z), :] = reach_low
    spread(mat_out.at[2], response)
    spread(mat_out.at[3], reach_high)

    loads[2].wait()
    for z in range(depth):
        halo_out[0, pl.ds(z, 1), :] = warmth[pl.ds(16 * z, 1), :]
        halo_out[1, pl.ds(z, 1), :] = warmth[pl.ds(16 * z + 15, 1), :]

    others = jnp.where(solving, solvers - 1, solvers)
    pl.semaphore_wait(barrier, others + has_low.astype(jnp.int32) + has_high.astype(jnp.int32))

    to_low = functools.partial(
        pltpu.make_async_remote_copy,
        halo_out.at[0],
        halo_high,
        send_sem.at[0],
        recv_sem.at[0],
        device_id_type=MESH,
    )
    to_high = functools.partial(
        pltpu.make_async_remote_copy,
        halo_out.at[1],
        halo_low,
        send_sem.at[1],
        recv_sem.at[1],
        device_id_type=MESH,
    )

    @pl.when(has_low)
    def _():
        to_low(device_id=(row - 1, me)).start()

    @pl.when(has_high)
    def _():
        to_high(device_id=(row + 1, me)).start()

    @pl.when(jnp.logical_not(has_low))
    def _():
        halo_low[...] = jnp.zeros_like(halo_low)

    @pl.when(jnp.logical_not(has_high))
    def _():
        halo_high[...] = jnp.zeros_like(halo_high)

    def scatter(out, into, which):
        own = pltpu.make_async_copy(
            out.at[:, pl.ds(my_solver * g_size, g_size)],
            into.at[:, pl.ds(me * g_size, g_size)],
            own_sem.at[which],
        )

        for s, target in enumerate(PLACES):

            @pl.when(target != me)
            def _():
                pltpu.make_async_remote_copy(
                    out.at[:, pl.ds(s * g_size, g_size)],
                    into.at[:, pl.ds(me * g_size, g_size)],
                    send_sem.at[2 + which],
                    recv_sem.at[2 + which],
                    device_id=(row, target),
                    device_id_type=MESH,
                ).start()

        @pl.when(solving)
        def _():
            own.start()

        return own

    def drain(ref, sem, count):
        part = ref.at[:, pl.ds(0, count)]
        pltpu.make_async_copy(part, part, sem).wait()

    own_matrix = scatter(mat_out, mat_in, 0)

    for copy in [loads[3], loads[4]] + smalls:
        copy.wait()
    kind = group[...]
    share = jnp.zeros((16, 256), jnp.float32)
    for c in range(ratio.shape[0]):
        share = jnp.where(kind == c, transverse_speed * ratio[c], share)
    row_at = lax.broadcasted_iota(jnp.int32, (16, 256), 0)
    lane_at = lax.broadcasted_iota(jnp.int32, (16, 256), 1)
    centre = (1.0 - 4.0 * mixing_coefficient) - share
    share_low = jnp.where(row_at == 0, 0.0, share)
    mixing_low = jnp.where(row_at == 0, 0.0, mixing_coefficient)
    share_high = jnp.where(row_at == 15, 0.0, share)
    mixing_high = jnp.where(row_at == 15, 0.0, mixing_coefficient)
    mixing_left = jnp.where(lane_at == 0, 0.0, mixing_coefficient)
    mixing_right = jnp.where(lane_at == 255, 0.0, mixing_coefficient)

    def direction(z):
        return sense[region[z]].astype(jnp.float32)

    for z in range(depth):
        forward = direction(z)
        here = warmth[slab(z), :]
        rhs[slab(z), :] = (
            centre * here
            + (mixing_low + forward * share_low) * pltpu.roll(here, 1, 0)
            + (mixing_high + (1.0 - forward) * share_high) * pltpu.roll(here, 15, 0)
            + mixing_left * pltpu.roll(here, 1, 1)
            + mixing_right * pltpu.roll(here, 255, 1)
            + supplied_power * supply[slab(z), :]
        )

    first_value = scale[slab(0), :] * rhs[slab(0), :]
    value = first_value
    for z in range(1, last):
        value = scale[slab(z), :] * rhs[slab(z), :] + low_scale[slab(z), :] * value
        part[slab(z), :] = value
    spread(rhs_out.at[0], (rhs[slab(last), :] + low_last * value) * inverse_high)
    for z in reversed(range(1, last - 1)):
        value = part[slab(z), :] + gain[slab(z), :] * value
    spread(rhs_out.at[1], first_value + gain[slab(0), :] * value)
    own_rhs = scatter(rhs_out, rhs_in, 1)

    @pl.when(has_high)
    def _():
        to_low(device_id=(row, me)).wait_recv()

    @pl.when(has_low)
    def _():
        to_high(device_id=(row, me)).wait_recv()

    edge_share_low = share[0:8, :] - share_low[0:8, :]
    edge_mixing_low = mixing_coefficient - mixing_low[0:8, :]
    edge_share_high = share[8:16, :] - share_high[8:16, :]
    edge_mixing_high = mixing_coefficient - mixing_high[8:16, :]

    def whole_rhs(z):
        forward = direction(z)
        low_row = (edge_mixing_low + forward * edge_share_low) * halo_low[pl.ds(z, 1), :]
        high_row = (edge_mixing_high + (1.0 - forward) * edge_share_high) * halo_high[pl.ds(z, 1), :]
        return rhs[slab(z), :] + jnp.concatenate([low_row, high_row], axis=0)

    def sides(ref, value):
        for h in range(4):
            x, half = 15 * (h // 2), LANES * (h % 2)
            ref[pl.ds(h, 1), :] = value[x : x + 1, half : half + LANES]

    value = jnp.zeros((16, 256), jnp.float32)
    for z in range(last):
        value = scale[slab(z), :] * whole_rhs(z) + low_scale[slab(z), :] * value
        rhs[slab(z), :] = value
    sides(side_rhs_out.at[0], (whole_rhs(last) + low_last * value) * inverse_high)
    for z in reversed(range(last - 1)):
        value = rhs[slab(z), :] + gain[slab(z), :] * value
        rhs[slab(z), :] = value
    sides(side_rhs_out.at[1], value)
    own_side = pltpu.make_async_copy(
        side_rhs_out.at[:, pl.ds(my_side, 1)], side_rhs_in.at[:, pl.ds(me, 1)], own_sem.at[3]
    )

    for h, s in enumerate(SIDES):
        target = PLACES[s]

        @pl.when(target != me)
        def _():
            pltpu.make_async_remote_copy(
                side_rhs_out.at[:, pl.ds(h, 1)],
                side_rhs_in.at[:, pl.ds(me, 1)],
                send_sem.at[5],
                recv_sem.at[5],
                device_id=(row, target),
                device_id_type=MESH,
            ).start()

    @pl.when(siding)
    def _():
        own_side.start()

    lines = axial * g_size
    def send_back(j, carry):
        @pl.when(j != me)
        def _():
            pltpu.make_async_remote_copy(
                edge_out.at[:, pl.ds(j * g_size, g_size)],
                edge_in.at[:, pl.ds(my_solver * g_size, g_size)],
                send_sem.at[4],
                recv_sem.at[4],
                device_id=(row, j),
                device_id_type=MESH,
            ).start()

        return carry

    own_back = pltpu.make_async_copy(
        edge_out.at[:, pl.ds(me * g_size, g_size)],
        edge_in.at[:, pl.ds(my_solver * g_size, g_size)],
        own_sem.at[2],
    )

    @pl.when(solving)
    def _():
        at = lax.broadcasted_iota(jnp.int32, (lines, LANES), 0)

        def down(x, blocks):
            return pltpu.roll(x, blocks * g_size, 0)

        def up(x, blocks):
            return pltpu.roll(x, lines - blocks * g_size, 0)

        is_first = at < g_size
        is_last = at >= lines - g_size
        drain(mat_in, recv_sem.at[2], (axial - 1) * g_size)
        own_matrix.wait()
        low = mat_in[0]
        excess = mat_in[1] + jnp.where(is_last, 1.0, up(mat_in[2], 1))
        high = jnp.where(is_last, 0.0, up(mat_in[3], 1))
        excess = jnp.where(is_first, excess + low, excess)
        low = jnp.where(is_first, 0.0, low)
        level, stride = 0, 1
        while stride < axial:
            inverse = 1.0 / (low + excess + high)
            a = low * down(inverse, stride)
            b = high * up(inverse, stride)
            alpha[level] = a
            beta[level] = b
            excess = excess + a * down(excess, stride) + b * up(excess, stride)
            low = a * down(low, stride)
            high = b * up(high, stride)
            level, stride = level + 1, stride * 2
        final = 1.0 / excess
        finals[...] = final

        drain(rhs_in, recv_sem.at[3], (axial - 1) * g_size)
        own_rhs.wait()
        r = rhs_in[0] + jnp.where(is_last, 0.0, up(rhs_in[1], 1))
        level, stride = 0, 1
        while stride < axial:
            r = r + alpha[level] * down(r, stride) + beta[level] * up(r, stride)
            level, stride = level + 1, stride * 2
        r = r * final
        edge_out[1] = r
        edge_out[0] = jnp.where(is_first, 0.0, down(r, 1))

        lax.fori_loop(0, RING_Y, send_back, 0)
        own_back.start()

    own_side_back = pltpu.make_async_copy(
        side_edge_out.at[:, pl.ds(me, 1)], side_edge_in.at[:, pl.ds(my_side, 1)], own_sem.at[4]
    )

    @pl.when(siding)
    def _():
        at = lax.broadcasted_iota(jnp.int32, (axial, LANES), 0)

        def down(x, blocks):
            return pltpu.roll(x, blocks, 0)

        def up(x, blocks):
            return pltpu.roll(x, axial - blocks, 0)

        local = (g_size - 1) * (my_side // 2)
        levels = alpha.shape[0]
        for level in range(levels):
            side_alpha[level] = alpha[level, pl.ds(local, axial, stride=g_size), :]
            side_beta[level] = beta[level, pl.ds(local, axial, stride=g_size), :]
        final = finals[pl.ds(local, axial, stride=g_size), :]
        drain(side_rhs_in, recv_sem.at[5], axial - 1)
        own_side.wait()
        r = side_rhs_in[0] + jnp.where(at == axial - 1, 0.0, up(side_rhs_in[1], 1))
        level, stride = 0, 1
        while stride < axial:
            r = r + side_alpha[level] * down(r, stride) + side_beta[level] * up(r, stride)
            level, stride = level + 1, stride * 2
        r = r * final
        side_edge_out[1] = r
        side_edge_out[0] = jnp.where(at == 0, 0.0, down(r, 1))

        def send(j, carry):
            @pl.when(j != me)
            def _():
                pltpu.make_async_remote_copy(
                    side_edge_out.at[:, pl.ds(j, 1)],
                    side_edge_in.at[:, pl.ds(my_side, 1)],
                    send_sem.at[6],
                    recv_sem.at[6],
                    device_id=(row, j),
                    device_id_type=MESH,
                ).start()

            return carry

        lax.fori_loop(0, axial, send, 0)
        own_side_back.start()

    @pl.when(solving)
    def _():
        lax.fori_loop(RING_Y, axial, send_back, 0)

    @pl.when(siding)
    def _():
        own_side_back.wait()
        drain(side_edge_in, recv_sem.at[6], len(SIDES) - 1)

    @pl.when(jnp.logical_not(siding))
    def _():
        drain(side_edge_in, recv_sem.at[6], len(SIDES))

    @pl.when(solving)
    def _():
        own_back.wait()
        drain(edge_in, recv_sem.at[4], axial - g_size)

    @pl.when(jnp.logical_not(solving))
    def _():
        drain(edge_in, recv_sem.at[4], axial)

    for k in range(2):
        for h, g in enumerate(BESIDE):
            edge_in[k, pl.ds(g, 1), :] = side_edge_in[k, pl.ds(h, 1), :]

    below_edge = gathered(edge_in.at[0])
    own_edge = gathered(edge_in.at[1])
    for z in range(last):
        out_ref[slab(z), :] = (
            rhs[slab(z), :] + below[slab(z), :] * below_edge + above[slab(z), :] * own_edge
        )
    out_ref[slab(last), :] = own_edge

    @pl.when(has_low)
    def _():
        to_low(device_id=(row, me)).wait_send()

    @pl.when(has_high)
    def _():
        to_high(device_id=(row, me)).wait_send()

    @pl.when(solving)
    def _():
        drain(mat_out, send_sem.at[2], axial - g_size)
        drain(rhs_out, send_sem.at[3], axial - g_size)
        drain(edge_out, send_sem.at[4], (axial - 1) * g_size)

    @pl.when(jnp.logical_not(solving))
    def _():
        drain(mat_out, send_sem.at[2], axial)
        drain(rhs_out, send_sem.at[3], axial)

    @pl.when(siding)
    def _():
        drain(side_rhs_out, send_sem.at[5], len(SIDES) - 1)
        drain(side_edge_out, send_sem.at[6], axial - 1)

    @pl.when(jnp.logical_not(siding))
    def _():
        drain(side_rhs_out, send_sem.at[5], len(SIDES))


def solution(mesh):
    axial, rows = mesh.shape["axial"], mesh.shape["row"]

    def on_device(warmth, supply, lower, higher, ratio, group, region, sense):
        depth, width, length = warmth.shape
        flat = (depth * width, length)
        lines = axial * (axial // len(PLACES))
        levels = axial.bit_length() - 1
        field = pltpu.VMEM(flat, jnp.float32)
        halo = pltpu.VMEM((depth, length), jnp.float32)
        out = pl.pallas_call(
            functools.partial(kernel, axial, rows, depth),
            out_shape=jax.ShapeDtypeStruct(flat, jnp.float32),
            in_specs=[pl.BlockSpec(memory_space=pltpu.HBM)] * 8,
            out_specs=pl.BlockSpec(memory_space=pltpu.VMEM),
            scratch_shapes=[
                field,
                field,
                field,
                field,
                pltpu.VMEM(group.shape, jnp.int32),
                pltpu.SMEM(ratio.shape, jnp.float32),
                pltpu.SMEM(region.shape, jnp.int32),
                pltpu.SMEM(sense.shape, jnp.int32),
                field,
                field,
                field,
                field,
                field,
                field,
                field,
                field,
                pltpu.VMEM((2, depth, length), jnp.float32),
                halo,
                halo,
                pltpu.VMEM((4, axial, LANES), jnp.float32),
                pltpu.VMEM((4, lines, LANES), jnp.float32),
                pltpu.VMEM((2, axial, LANES), jnp.float32),
                pltpu.VMEM((2, lines, LANES), jnp.float32),
                pltpu.VMEM((2, lines, LANES), jnp.float32),
                pltpu.VMEM((2, axial, LANES), jnp.float32),
                pltpu.VMEM((2, len(SIDES), LANES), jnp.float32),
                pltpu.VMEM((2, axial, LANES), jnp.float32),
                pltpu.VMEM((2, axial, LANES), jnp.float32),
                pltpu.VMEM((2, len(SIDES), LANES), jnp.float32),
                pltpu.VMEM((levels, lines, LANES), jnp.float32),
                pltpu.VMEM((levels, lines, LANES), jnp.float32),
                pltpu.VMEM((levels, axial, LANES), jnp.float32),
                pltpu.VMEM((levels, axial, LANES), jnp.float32),
                pltpu.VMEM((lines, LANES), jnp.float32),
                pltpu.SemaphoreType.DMA((5,)),
                pltpu.SemaphoreType.DMA((3,)),
                pltpu.SemaphoreType.DMA((5,)),
                pltpu.SemaphoreType.DMA((7,)),
                pltpu.SemaphoreType.DMA((7,)),
            ],
            compiler_params=pltpu.CompilerParams(
                collective_id=0, has_side_effects=True, vmem_limit_bytes=32 * 1024 * 1024
            ),
        )(
            *(
                pltpu.with_memory_space_constraint(x, pltpu.HBM)
                for x in (
                    warmth.reshape(flat),
                    supply.reshape(flat),
                    lower.reshape(flat),
                    higher.reshape(flat),
                    ratio,
                    group,
                    region,
                    sense,
                )
            )
        )
        return out.reshape(warmth.shape)

    placed = (
        P("axial", "row", None),
        P("axial", "row", None),
        P("axial", "row", None),
        P("axial", "row", None),
        P(),
        P("row", None),
        P("axial"),
        P(),
    )
    return jax.shard_map(
        on_device, mesh=mesh, in_specs=placed, out_specs=P("axial", "row", None), check_vma=False
    )
```

```python
import functools

import jax
import jax.numpy as jnp
from jax import lax
from jax.experimental import pallas as pl
from jax.experimental.pallas import tpu as pltpu
from jax.sharding import PartitionSpec as P

transverse_speed = 0.35
mixing_coefficient = 0.15
supplied_power = 0.5
axial_drift = 64.0

MESH = pl.DeviceIdType.MESH
LANES = 128
RING_Y = 4
PLACES = (0, 8, 1, 9, 12, 4, 13, 5)
BESIDE = (0, 8, 23, 31)
SIDES = (0, 2, 5, 7)


def spread(ref, value):
    for a in range(2):
        for b in range(2):
            ref[pl.ds(8 * (2 * a + b), 8), :] = value[8 * a : 8 * a + 8, LANES * b : LANES * (b + 1)]


def gathered(ref):
    parts = [ref[pl.ds(8 * t, 8), :] for t in range(4)]
    return jnp.concatenate(
        [jnp.concatenate(parts[:2], axis=1), jnp.concatenate(parts[2:], axis=1)], axis=0
    )


def kernel(
    axial,
    rows,
    depth,
    warmth_hbm,
    supply_hbm,
    lower_hbm,
    higher_hbm,
    ratio_hbm,
    group_hbm,
    region_hbm,
    sense_hbm,
    out_ref,
    warmth,
    supply,
    lower,
    higher,
    group,
    ratio,
    region,
    sense,
    gain,
    scale,
    low_scale,
    below,
    above,
    unit,
    rhs,
    part,
    halo_out,
    halo_low,
    halo_high,
    mat_out,
    mat_in,
    rhs_out,
    rhs_in,
    edge_out,
    edge_in,
    side_rhs_out,
    side_rhs_in,
    side_edge_out,
    side_edge_in,
    alpha,
    beta,
    side_alpha,
    side_beta,
    finals,
    load_sem,
    small_sem,
    own_sem,
    send_sem,
    recv_sem,
):
    me = lax.axis_index("axial")
    row = lax.axis_index("row")
    solvers = len(PLACES)
    g_size = axial // solvers
    my_solver = sum((me == place).astype(jnp.int32) * s for s, place in enumerate(PLACES))
    solving = sum((me == place).astype(jnp.int32) for place in PLACES) > 0
    my_side = sum((me == PLACES[s]).astype(jnp.int32) * h for h, s in enumerate(SIDES))
    kept_size = g_size - 1
    skipped = 1 - my_side // 2
    siding = sum((me == PLACES[s]).astype(jnp.int32) for s in SIDES) > 0
    has_low = row > 0
    has_high = row < rows - 1

    barrier = pltpu.get_barrier_semaphore()

    @pl.when(has_low)
    def _():
        pl.semaphore_signal(barrier, inc=1, device_id=(row - 1, me), device_id_type=MESH)

    @pl.when(has_high)
    def _():
        pl.semaphore_signal(barrier, inc=1, device_id=(row + 1, me), device_id_type=MESH)

    def greet(j, carry):
        @pl.when(j != me)
        def _():
            pl.semaphore_signal(barrier, inc=1, device_id=(row, j), device_id_type=MESH)

        return carry

    @pl.when(siding)
    def _():
        rhs_in[...] = jnp.zeros_like(rhs_in)

    @pl.when(solving)
    def _():
        lax.fori_loop(0, axial, lambda i, c: greet(axial - 1 - i, c), 0)

    loads = [
        pltpu.make_async_copy(source, target, load_sem.at[i])
        for i, (source, target) in enumerate(
            [
                (higher_hbm, higher),
                (lower_hbm, lower),
                (warmth_hbm, warmth),
                (supply_hbm, supply),
                (group_hbm, group),
            ]
        )
    ]
    smalls = [
        pltpu.make_async_copy(source, target, small_sem.at[i])
        for i, (source, target) in enumerate(
            [(ratio_hbm, ratio), (region_hbm, region), (sense_hbm, sense)]
        )
    ]
    for copy in loads + smalls:
        copy.start()

    def slab(z):
        return pl.ds(16 * z, 16)

    loads[0].wait()
    loads[1].wait()
    kept = jnp.ones((16, 256), jnp.float32)
    weight = jnp.ones((16, 256), jnp.float32)
    source = jnp.zeros((16, 256), jnp.float32)
    last = depth - 1
    for z in range(last):
        low = lower[slab(z), :] + axial_drift
        high = higher[slab(z), :]
        excess = 1.0 + low * kept
        inverse = 1.0 / (excess + high)
        low_ratio = low * inverse
        gain[slab(z), :] = high * inverse
        scale[slab(z), :] = inverse
        low_scale[slab(z), :] = low_ratio
        kept = excess * inverse
        weight = low_ratio * weight
        source = inverse + low_ratio * source
        below[slab(z), :] = weight
        unit[slab(z), :] = source
    low_last = lower[slab(last), :] + axial_drift
    inverse_high = 1.0 / higher[slab(last), :]
    spread(mat_out.at[0], low_last * weight * inverse_high)
    spread(mat_out.at[1], (1.0 + low_last * source) * inverse_high)
    reach_low = weight
    reach_high = gain[slab(last - 1), :]
    response = source
    above[slab(last - 1), :] = reach_high
    for z in reversed(range(last - 1)):
        factor = gain[slab(z), :]
        reach_high = factor * reach_high
        reach_low = below[slab(z), :] + factor * reach_low
        response = unit[slab(z), :] + factor * response
        above[slab(z), :] = reach_high
        below[slab(z), :] = reach_low
    spread(mat_out.at[2], response)
    spread(mat_out.at[3], reach_high)

    loads[2].wait()
    for z in range(depth):
        halo_out[0, pl.ds(z, 1), :] = warmth[pl.ds(16 * z, 1), :]
        halo_out[1, pl.ds(z, 1), :] = warmth[pl.ds(16 * z + 15, 1), :]

    others = jnp.where(solving, solvers - 1, solvers)
    pl.semaphore_wait(barrier, others + has_low.astype(jnp.int32) + has_high.astype(jnp.int32))

    to_low = functools.partial(
        pltpu.make_async_remote_copy,
        halo_out.at[0],
        halo_high,
        send_sem.at[0],
        recv_sem.at[0],
        device_id_type=MESH,
    )
    to_high = functools.partial(
        pltpu.make_async_remote_copy,
        halo_out.at[1],
        halo_low,
        send_sem.at[1],
        recv_sem.at[1],
        device_id_type=MESH,
    )

    @pl.when(has_low)
    def _():
        to_low(device_id=(row - 1, me)).start()

    @pl.when(has_high)
    def _():
        to_high(device_id=(row + 1, me)).start()

    @pl.when(jnp.logical_not(has_low))
    def _():
        halo_low[...] = jnp.zeros_like(halo_low)

    @pl.when(jnp.logical_not(has_high))
    def _():
        halo_high[...] = jnp.zeros_like(halo_high)

    def scatter(out, into, which):
        own = pltpu.make_async_copy(
            out.at[:, pl.ds(my_solver * g_size, g_size)],
            into.at[:, pl.ds(me * g_size, g_size)],
            own_sem.at[which],
        )

        for s, target in enumerate(PLACES):
            first, size = 0, g_size
            if which == 1 and s in SIDES:
                first, size = 1 - SIDES.index(s) // 2, kept_size

            @pl.when(target != me)
            def _():
                pltpu.make_async_remote_copy(
                    out.at[:, pl.ds(s * g_size + first, size)],
                    into.at[:, pl.ds(me * g_size + first, size)],
                    send_sem.at[2 + which],
                    recv_sem.at[2 + which],
                    device_id=(row, target),
                    device_id_type=MESH,
                ).start()

        @pl.when(solving)
        def _():
            own.start()

        return own

    def drain(ref, sem, count):
        part = ref.at[:, pl.ds(0, count)]
        pltpu.make_async_copy(part, part, sem).wait()

    plain = jnp.logical_and(solving, jnp.logical_not(siding))
    total = axial - len(SIDES)

    def by_role(ref, sem, side_count, plain_count, other_count=None):
        @pl.when(siding)
        def _():
            drain(ref, sem, side_count)

        @pl.when(plain)
        def _():
            drain(ref, sem, plain_count)

        if other_count is not None:

            @pl.when(jnp.logical_not(solving))
            def _():
                drain(ref, sem, other_count)

    own_matrix = scatter(mat_out, mat_in, 0)

    for copy in [loads[3], loads[4]] + smalls:
        copy.wait()
    kind = group[...]
    share = jnp.zeros((16, 256), jnp.float32)
    for c in range(ratio.shape[0]):
        share = jnp.where(kind == c, transverse_speed * ratio[c], share)
    row_at = lax.broadcasted_iota(jnp.int32, (16, 256), 0)
    lane_at = lax.broadcasted_iota(jnp.int32, (16, 256), 1)
    centre = (1.0 - 4.0 * mixing_coefficient) - share
    share_low = jnp.where(row_at == 0, 0.0, share)
    mixing_low = jnp.where(row_at == 0, 0.0, mixing_coefficient)
    share_high = jnp.where(row_at == 15, 0.0, share)
    mixing_high = jnp.where(row_at == 15, 0.0, mixing_coefficient)
    mixing_left = jnp.where(lane_at == 0, 0.0, mixing_coefficient)
    mixing_right = jnp.where(lane_at == 255, 0.0, mixing_coefficient)

    def direction(z):
        return sense[region[z]].astype(jnp.float32)

    for z in range(depth):
        forward = direction(z)
        here = warmth[slab(z), :]
        rhs[slab(z), :] = (
            centre * here
            + (mixing_low + forward * share_low) * pltpu.roll(here, 1, 0)
            + (mixing_high + (1.0 - forward) * share_high) * pltpu.roll(here, 15, 0)
            + mixing_left * pltpu.roll(here, 1, 1)
            + mixing_right * pltpu.roll(here, 255, 1)
            + supplied_power * supply[slab(z), :]
        )

    first_value = scale[slab(0), :] * rhs[slab(0), :]
    value = first_value
    for z in range(1, last):
        value = scale[slab(z), :] * rhs[slab(z), :] + low_scale[slab(z), :] * value
        part[slab(z), :] = value
    spread(rhs_out.at[0], (rhs[slab(last), :] + low_last * value) * inverse_high)
    for z in reversed(range(1, last - 1)):
        value = part[slab(z), :] + gain[slab(z), :] * value
    spread(rhs_out.at[1], first_value + gain[slab(0), :] * value)
    own_rhs = scatter(rhs_out, rhs_in, 1)

    @pl.when(has_high)
    def _():
        to_low(device_id=(row, me)).wait_recv()

    @pl.when(has_low)
    def _():
        to_high(device_id=(row, me)).wait_recv()

    edge_share_low = share[0:8, :] - share_low[0:8, :]
    edge_mixing_low = mixing_coefficient - mixing_low[0:8, :]
    edge_share_high = share[8:16, :] - share_high[8:16, :]
    edge_mixing_high = mixing_coefficient - mixing_high[8:16, :]

    def whole_rhs(z):
        forward = direction(z)
        low_row = (edge_mixing_low + forward * edge_share_low) * halo_low[pl.ds(z, 1), :]
        high_row = (edge_mixing_high + (1.0 - forward) * edge_share_high) * halo_high[pl.ds(z, 1), :]
        return rhs[slab(z), :] + jnp.concatenate([low_row, high_row], axis=0)

    def sides(ref, value):
        for h in range(4):
            x, half = 15 * (h // 2), LANES * (h % 2)
            ref[pl.ds(h, 1), :] = value[x : x + 1, half : half + LANES]

    value = jnp.zeros((16, 256), jnp.float32)
    for z in range(last):
        value = scale[slab(z), :] * whole_rhs(z) + low_scale[slab(z), :] * value
        rhs[slab(z), :] = value
    sides(side_rhs_out.at[0], (whole_rhs(last) + low_last * value) * inverse_high)
    for z in reversed(range(last - 1)):
        value = rhs[slab(z), :] + gain[slab(z), :] * value
        rhs[slab(z), :] = value
    sides(side_rhs_out.at[1], value)
    own_side = pltpu.make_async_copy(
        side_rhs_out.at[:, pl.ds(my_side, 1)], side_rhs_in.at[:, pl.ds(me, 1)], own_sem.at[3]
    )

    for h, s in enumerate(SIDES):
        target = PLACES[s]

        @pl.when(target != me)
        def _():
            pltpu.make_async_remote_copy(
                side_rhs_out.at[:, pl.ds(h, 1)],
                side_rhs_in.at[:, pl.ds(me, 1)],
                send_sem.at[5],
                recv_sem.at[5],
                device_id=(row, target),
                device_id_type=MESH,
            ).start()

    @pl.when(siding)
    def _():
        own_side.start()

    lines = axial * g_size
    def send_back(first, size, j, carry):
        @pl.when(j != me)
        def _():
            pltpu.make_async_remote_copy(
                edge_out.at[:, pl.ds(j * g_size + first, size)],
                edge_in.at[:, pl.ds(my_solver * g_size + first, size)],
                send_sem.at[4],
                recv_sem.at[4],
                device_id=(row, j),
                device_id_type=MESH,
            ).start()

        return carry

    def send_back_to(start, stop):
        @pl.when(siding)
        def _():
            lax.fori_loop(start, stop, functools.partial(send_back, skipped, kept_size), 0)

        @pl.when(plain)
        def _():
            lax.fori_loop(start, stop, functools.partial(send_back, 0, g_size), 0)

    own_back = pltpu.make_async_copy(
        edge_out.at[:, pl.ds(me * g_size, g_size)],
        edge_in.at[:, pl.ds(my_solver * g_size, g_size)],
        own_sem.at[2],
    )

    @pl.when(solving)
    def _():
        at = lax.broadcasted_iota(jnp.int32, (lines, LANES), 0)

        def down(x, blocks):
            return pltpu.roll(x, blocks * g_size, 0)

        def up(x, blocks):
            return pltpu.roll(x, lines - blocks * g_size, 0)

        is_first = at < g_size
        is_last = at >= lines - g_size
        drain(mat_in, recv_sem.at[2], (axial - 1) * g_size)
        own_matrix.wait()
        low = mat_in[0]
        excess = mat_in[1] + jnp.where(is_last, 1.0, up(mat_in[2], 1))
        high = jnp.where(is_last, 0.0, up(mat_in[3], 1))
        excess = jnp.where(is_first, excess + low, excess)
        low = jnp.where(is_first, 0.0, low)
        level, stride = 0, 1
        while stride < axial:
            inverse = 1.0 / (low + excess + high)
            a = low * down(inverse, stride)
            b = high * up(inverse, stride)
            alpha[level] = a
            beta[level] = b
            excess = excess + a * down(excess, stride) + b * up(excess, stride)
            low = a * down(low, stride)
            high = b * up(high, stride)
            level, stride = level + 1, stride * 2
        final = 1.0 / excess
        finals[...] = final

        by_role(rhs_in, recv_sem.at[3], (axial - 1) * kept_size, (axial - 1) * g_size)
        own_rhs.wait()
        r = rhs_in[0] + jnp.where(is_last, 0.0, up(rhs_in[1], 1))
        level, stride = 0, 1
        while stride < axial:
            r = r + alpha[level] * down(r, stride) + beta[level] * up(r, stride)
            level, stride = level + 1, stride * 2
        r = r * final
        edge_out[1] = r
        edge_out[0] = jnp.where(is_first, 0.0, down(r, 1))

        send_back_to(0, RING_Y)
        own_back.start()

    own_side_back = pltpu.make_async_copy(
        side_edge_out.at[:, pl.ds(me, 1)], side_edge_in.at[:, pl.ds(my_side, 1)], own_sem.at[4]
    )

    @pl.when(siding)
    def _():
        at = lax.broadcasted_iota(jnp.int32, (axial, LANES), 0)

        def down(x, blocks):
            return pltpu.roll(x, blocks, 0)

        def up(x, blocks):
            return pltpu.roll(x, axial - blocks, 0)

        local = (g_size - 1) * (my_side // 2)
        levels = alpha.shape[0]
        for level in range(levels):
            side_alpha[level] = alpha[level, pl.ds(local, axial, stride=g_size), :]
            side_beta[level] = beta[level, pl.ds(local, axial, stride=g_size), :]
        final = finals[pl.ds(local, axial, stride=g_size), :]
        drain(side_rhs_in, recv_sem.at[5], axial - 1)
        own_side.wait()
        r = side_rhs_in[0] + jnp.where(at == axial - 1, 0.0, up(side_rhs_in[1], 1))
        level, stride = 0, 1
        while stride < axial:
            r = r + side_alpha[level] * down(r, stride) + side_beta[level] * up(r, stride)
            level, stride = level + 1, stride * 2
        r = r * final
        side_edge_out[1] = r
        side_edge_out[0] = jnp.where(at == 0, 0.0, down(r, 1))

        def send(j, carry):
            @pl.when(j != me)
            def _():
                pltpu.make_async_remote_copy(
                    side_edge_out.at[:, pl.ds(j, 1)],
                    side_edge_in.at[:, pl.ds(my_side, 1)],
                    send_sem.at[6],
                    recv_sem.at[6],
                    device_id=(row, j),
                    device_id_type=MESH,
                ).start()

            return carry

        lax.fori_loop(0, axial, send, 0)
        own_side_back.start()

    send_back_to(RING_Y, axial)

    @pl.when(siding)
    def _():
        own_side_back.wait()
        drain(side_edge_in, recv_sem.at[6], len(SIDES) - 1)

    @pl.when(jnp.logical_not(siding))
    def _():
        drain(side_edge_in, recv_sem.at[6], len(SIDES))

    by_role(edge_in, recv_sem.at[4], total - kept_size, total - g_size, total)

    @pl.when(solving)
    def _():
        own_back.wait()

    for k in range(2):
        for h, g in enumerate(BESIDE):
            edge_in[k, pl.ds(g, 1), :] = side_edge_in[k, pl.ds(h, 1), :]

    below_edge = gathered(edge_in.at[0])
    own_edge = gathered(edge_in.at[1])
    for z in range(last):
        out_ref[slab(z), :] = (
            rhs[slab(z), :] + below[slab(z), :] * below_edge + above[slab(z), :] * own_edge
        )
    out_ref[slab(last), :] = own_edge

    @pl.when(has_low)
    def _():
        to_low(device_id=(row, me)).wait_send()

    @pl.when(has_high)
    def _():
        to_high(device_id=(row, me)).wait_send()

    by_role(mat_out, send_sem.at[2], axial - g_size, axial - g_size, axial)
    by_role(rhs_out, send_sem.at[3], total - kept_size, total - g_size, total)
    by_role(edge_out, send_sem.at[4], (axial - 1) * kept_size, (axial - 1) * g_size)

    @pl.when(siding)
    def _():
        drain(side_rhs_out, send_sem.at[5], len(SIDES) - 1)
        drain(side_edge_out, send_sem.at[6], axial - 1)

    @pl.when(jnp.logical_not(siding))
    def _():
        drain(side_rhs_out, send_sem.at[5], len(SIDES))


def solution(mesh):
    axial, rows = mesh.shape["axial"], mesh.shape["row"]

    def on_device(warmth, supply, lower, higher, ratio, group, region, sense):
        depth, width, length = warmth.shape
        flat = (depth * width, length)
        lines = axial * (axial // len(PLACES))
        levels = axial.bit_length() - 1
        field = pltpu.VMEM(flat, jnp.float32)
        halo = pltpu.VMEM((depth, length), jnp.float32)
        out = pl.pallas_call(
            functools.partial(kernel, axial, rows, depth),
            out_shape=jax.ShapeDtypeStruct(flat, jnp.float32),
            in_specs=[pl.BlockSpec(memory_space=pltpu.HBM)] * 8,
            out_specs=pl.BlockSpec(memory_space=pltpu.VMEM),
            scratch_shapes=[
                field,
                field,
                field,
                field,
                pltpu.VMEM(group.shape, jnp.int32),
                pltpu.SMEM(ratio.shape, jnp.float32),
                pltpu.SMEM(region.shape, jnp.int32),
                pltpu.SMEM(sense.shape, jnp.int32),
                field,
                field,
                field,
                field,
                field,
                field,
                field,
                field,
                pltpu.VMEM((2, depth, length), jnp.float32),
                halo,
                halo,
                pltpu.VMEM((4, axial, LANES), jnp.float32),
                pltpu.VMEM((4, lines, LANES), jnp.float32),
                pltpu.VMEM((2, axial, LANES), jnp.float32),
                pltpu.VMEM((2, lines, LANES), jnp.float32),
                pltpu.VMEM((2, lines, LANES), jnp.float32),
                pltpu.VMEM((2, axial, LANES), jnp.float32),
                pltpu.VMEM((2, len(SIDES), LANES), jnp.float32),
                pltpu.VMEM((2, axial, LANES), jnp.float32),
                pltpu.VMEM((2, axial, LANES), jnp.float32),
                pltpu.VMEM((2, len(SIDES), LANES), jnp.float32),
                pltpu.VMEM((levels, lines, LANES), jnp.float32),
                pltpu.VMEM((levels, lines, LANES), jnp.float32),
                pltpu.VMEM((levels, axial, LANES), jnp.float32),
                pltpu.VMEM((levels, axial, LANES), jnp.float32),
                pltpu.VMEM((lines, LANES), jnp.float32),
                pltpu.SemaphoreType.DMA((5,)),
                pltpu.SemaphoreType.DMA((3,)),
                pltpu.SemaphoreType.DMA((5,)),
                pltpu.SemaphoreType.DMA((7,)),
                pltpu.SemaphoreType.DMA((7,)),
            ],
            compiler_params=pltpu.CompilerParams(
                collective_id=0, has_side_effects=True, vmem_limit_bytes=32 * 1024 * 1024
            ),
        )(
            *(
                pltpu.with_memory_space_constraint(x, pltpu.HBM)
                for x in (
                    warmth.reshape(flat),
                    supply.reshape(flat),
                    lower.reshape(flat),
                    higher.reshape(flat),
                    ratio,
                    group,
                    region,
                    sense,
                )
            )
        )
        return out.reshape(warmth.shape)

    placed = (
        P("axial", "row", None),
        P("axial", "row", None),
        P("axial", "row", None),
        P("axial", "row", None),
        P(),
        P("row", None),
        P("axial"),
        P(),
    )
    return jax.shard_map(
        on_device, mesh=mesh, in_specs=placed, out_specs=P("axial", "row", None), check_vma=False
    )
```

```python
import functools

import jax
import jax.numpy as jnp
from jax import lax
from jax.experimental import pallas as pl
from jax.experimental.pallas import tpu as pltpu
from jax.sharding import PartitionSpec as P

transverse_speed = 0.35
mixing_coefficient = 0.15
supplied_power = 0.5
axial_drift = 64.0

MESH = pl.DeviceIdType.MESH
LANES = 128
RING_Y = 4
PLACES = (4, 8, 5, 9, 12, 0, 13, 1)
BESIDE = (0, 8, 23, 31)
SIDES = (0, 2, 5, 7)


def spread(ref, value):
    for a in range(2):
        for b in range(2):
            ref[pl.ds(8 * (2 * a + b), 8), :] = value[8 * a : 8 * a + 8, LANES * b : LANES * (b + 1)]


def gathered(ref):
    parts = [ref[pl.ds(8 * t, 8), :] for t in range(4)]
    return jnp.concatenate(
        [jnp.concatenate(parts[:2], axis=1), jnp.concatenate(parts[2:], axis=1)], axis=0
    )


def kernel(
    axial,
    rows,
    depth,
    warmth_hbm,
    supply_hbm,
    lower_hbm,
    higher_hbm,
    ratio_hbm,
    group_hbm,
    region_hbm,
    sense_hbm,
    out_ref,
    warmth,
    supply,
    lower,
    higher,
    group,
    ratio,
    region,
    sense,
    gain,
    scale,
    low_scale,
    below,
    above,
    unit,
    rhs,
    part,
    halo_out,
    halo_low,
    halo_high,
    mat_out,
    mat_in,
    rhs_out,
    rhs_in,
    edge_out,
    edge_in,
    side_rhs_out,
    side_rhs_in,
    side_edge_out,
    side_edge_in,
    alpha,
    beta,
    side_alpha,
    side_beta,
    finals,
    load_sem,
    small_sem,
    own_sem,
    send_sem,
    recv_sem,
):
    me = lax.axis_index("axial")
    row = lax.axis_index("row")
    solvers = len(PLACES)
    g_size = axial // solvers
    my_solver = sum((me == place).astype(jnp.int32) * s for s, place in enumerate(PLACES))
    solving = sum((me == place).astype(jnp.int32) for place in PLACES) > 0
    my_side = sum((me == PLACES[s]).astype(jnp.int32) * h for h, s in enumerate(SIDES))
    kept_size = g_size - 1
    skipped = 1 - my_side // 2
    siding = sum((me == PLACES[s]).astype(jnp.int32) for s in SIDES) > 0
    has_low = row > 0
    has_high = row < rows - 1

    barrier = pltpu.get_barrier_semaphore()

    @pl.when(has_low)
    def _():
        pl.semaphore_signal(barrier, inc=1, device_id=(row - 1, me), device_id_type=MESH)

    @pl.when(has_high)
    def _():
        pl.semaphore_signal(barrier, inc=1, device_id=(row + 1, me), device_id_type=MESH)

    def greet(j, carry):
        @pl.when(j != me)
        def _():
            pl.semaphore_signal(barrier, inc=1, device_id=(row, j), device_id_type=MESH)

        return carry

    @pl.when(siding)
    def _():
        rhs_in[...] = jnp.zeros_like(rhs_in)

    @pl.when(solving)
    def _():
        lax.fori_loop(0, axial, lambda i, c: greet(axial - 1 - i, c), 0)

    loads = [
        pltpu.make_async_copy(source, target, load_sem.at[i])
        for i, (source, target) in enumerate(
            [
                (higher_hbm, higher),
                (lower_hbm, lower),
                (warmth_hbm, warmth),
                (supply_hbm, supply),
                (group_hbm, group),
            ]
        )
    ]
    smalls = [
        pltpu.make_async_copy(source, target, small_sem.at[i])
        for i, (source, target) in enumerate(
            [(ratio_hbm, ratio), (region_hbm, region), (sense_hbm, sense)]
        )
    ]
    for copy in loads + smalls:
        copy.start()

    def slab(z):
        return pl.ds(16 * z, 16)

    loads[0].wait()
    loads[1].wait()
    kept = jnp.ones((16, 256), jnp.float32)
    weight = jnp.ones((16, 256), jnp.float32)
    source = jnp.zeros((16, 256), jnp.float32)
    last = depth - 1
    for z in range(last):
        low = lower[slab(z), :] + axial_drift
        high = higher[slab(z), :]
        excess = 1.0 + low * kept
        inverse = 1.0 / (excess + high)
        low_ratio = low * inverse
        gain[slab(z), :] = high * inverse
        scale[slab(z), :] = inverse
        low_scale[slab(z), :] = low_ratio
        kept = excess * inverse
        weight = low_ratio * weight
        source = inverse + low_ratio * source
        below[slab(z), :] = weight
        unit[slab(z), :] = source
    low_last = lower[slab(last), :] + axial_drift
    inverse_high = 1.0 / higher[slab(last), :]
    spread(mat_out.at[0], low_last * weight * inverse_high)
    spread(mat_out.at[1], (1.0 + low_last * source) * inverse_high)
    reach_low = weight
    reach_high = gain[slab(last - 1), :]
    response = source
    above[slab(last - 1), :] = reach_high
    for z in reversed(range(last - 1)):
        factor = gain[slab(z), :]
        reach_high = factor * reach_high
        reach_low = below[slab(z), :] + factor * reach_low
        response = unit[slab(z), :] + factor * response
        above[slab(z), :] = reach_high
        below[slab(z), :] = reach_low
    spread(mat_out.at[2], response)
    spread(mat_out.at[3], reach_high)

    loads[2].wait()
    for z in range(depth):
        halo_out[0, pl.ds(z, 1), :] = warmth[pl.ds(16 * z, 1), :]
        halo_out[1, pl.ds(z, 1), :] = warmth[pl.ds(16 * z + 15, 1), :]

    others = jnp.where(solving, solvers - 1, solvers)
    pl.semaphore_wait(barrier, others + has_low.astype(jnp.int32) + has_high.astype(jnp.int32))

    to_low = functools.partial(
        pltpu.make_async_remote_copy,
        halo_out.at[0],
        halo_high,
        send_sem.at[0],
        recv_sem.at[0],
        device_id_type=MESH,
    )
    to_high = functools.partial(
        pltpu.make_async_remote_copy,
        halo_out.at[1],
        halo_low,
        send_sem.at[1],
        recv_sem.at[1],
        device_id_type=MESH,
    )

    @pl.when(has_low)
    def _():
        to_low(device_id=(row - 1, me)).start()

    @pl.when(has_high)
    def _():
        to_high(device_id=(row + 1, me)).start()

    @pl.when(jnp.logical_not(has_low))
    def _():
        halo_low[...] = jnp.zeros_like(halo_low)

    @pl.when(jnp.logical_not(has_high))
    def _():
        halo_high[...] = jnp.zeros_like(halo_high)

    def scatter(out, into, which):
        own = pltpu.make_async_copy(
            out.at[:, pl.ds(my_solver * g_size, g_size)],
            into.at[:, pl.ds(me * g_size, g_size)],
            own_sem.at[which],
        )

        for s, target in enumerate(PLACES):
            first, size = 0, g_size
            if which == 1 and s in SIDES:
                first, size = 1 - SIDES.index(s) // 2, kept_size

            @pl.when(target != me)
            def _():
                pltpu.make_async_remote_copy(
                    out.at[:, pl.ds(s * g_size + first, size)],
                    into.at[:, pl.ds(me * g_size + first, size)],
                    send_sem.at[2 + which],
                    recv_sem.at[2 + which],
                    device_id=(row, target),
                    device_id_type=MESH,
                ).start()

        @pl.when(solving)
        def _():
            own.start()

        return own

    def drain(ref, sem, count):
        part = ref.at[:, pl.ds(0, count)]
        pltpu.make_async_copy(part, part, sem).wait()

    plain = jnp.logical_and(solving, jnp.logical_not(siding))
    total = axial - len(SIDES)

    def by_role(ref, sem, side_count, plain_count, other_count=None):
        @pl.when(siding)
        def _():
            drain(ref, sem, side_count)

        @pl.when(plain)
        def _():
            drain(ref, sem, plain_count)

        if other_count is not None:

            @pl.when(jnp.logical_not(solving))
            def _():
                drain(ref, sem, other_count)

    own_matrix = scatter(mat_out, mat_in, 0)

    for copy in [loads[3], loads[4]] + smalls:
        copy.wait()
    kind = group[...]
    share = jnp.zeros((16, 256), jnp.float32)
    for c in range(ratio.shape[0]):
        share = jnp.where(kind == c, transverse_speed * ratio[c], share)
    row_at = lax.broadcasted_iota(jnp.int32, (16, 256), 0)
    lane_at = lax.broadcasted_iota(jnp.int32, (16, 256), 1)
    centre = (1.0 - 4.0 * mixing_coefficient) - share
    share_low = jnp.where(row_at == 0, 0.0, share)
    mixing_low = jnp.where(row_at == 0, 0.0, mixing_coefficient)
    share_high = jnp.where(row_at == 15, 0.0, share)
    mixing_high = jnp.where(row_at == 15, 0.0, mixing_coefficient)
    mixing_left = jnp.where(lane_at == 0, 0.0, mixing_coefficient)
    mixing_right = jnp.where(lane_at == 255, 0.0, mixing_coefficient)

    def direction(z):
        return sense[region[z]].astype(jnp.float32)

    for z in range(depth):
        forward = direction(z)
        here = warmth[slab(z), :]
        rhs[slab(z), :] = (
            centre * here
            + (mixing_low + forward * share_low) * pltpu.roll(here, 1, 0)
            + (mixing_high + (1.0 - forward) * share_high) * pltpu.roll(here, 15, 0)
            + mixing_left * pltpu.roll(here, 1, 1)
            + mixing_right * pltpu.roll(here, 255, 1)
            + supplied_power * supply[slab(z), :]
        )

    first_value = scale[slab(0), :] * rhs[slab(0), :]
    value = first_value
    for z in range(1, last):
        value = scale[slab(z), :] * rhs[slab(z), :] + low_scale[slab(z), :] * value
        part[slab(z), :] = value
    spread(rhs_out.at[0], (rhs[slab(last), :] + low_last * value) * inverse_high)
    for z in reversed(range(1, last - 1)):
        value = part[slab(z), :] + gain[slab(z), :] * value
    spread(rhs_out.at[1], first_value + gain[slab(0), :] * value)
    own_rhs = scatter(rhs_out, rhs_in, 1)

    @pl.when(has_high)
    def _():
        to_low(device_id=(row, me)).wait_recv()

    @pl.when(has_low)
    def _():
        to_high(device_id=(row, me)).wait_recv()

    edge_share_low = share[0:8, :] - share_low[0:8, :]
    edge_mixing_low = mixing_coefficient - mixing_low[0:8, :]
    edge_share_high = share[8:16, :] - share_high[8:16, :]
    edge_mixing_high = mixing_coefficient - mixing_high[8:16, :]

    def whole_rhs(z):
        forward = direction(z)
        low_row = (edge_mixing_low + forward * edge_share_low) * halo_low[pl.ds(z, 1), :]
        high_row = (edge_mixing_high + (1.0 - forward) * edge_share_high) * halo_high[pl.ds(z, 1), :]
        return rhs[slab(z), :] + jnp.concatenate([low_row, high_row], axis=0)

    def sides(ref, value):
        for h in range(4):
            x, half = 15 * (h // 2), LANES * (h % 2)
            ref[pl.ds(h, 1), :] = value[x : x + 1, half : half + LANES]

    value = jnp.zeros((16, 256), jnp.float32)
    for z in range(last):
        value = scale[slab(z), :] * whole_rhs(z) + low_scale[slab(z), :] * value
        rhs[slab(z), :] = value
    sides(side_rhs_out.at[0], (whole_rhs(last) + low_last * value) * inverse_high)
    for z in reversed(range(last - 1)):
        value = rhs[slab(z), :] + gain[slab(z), :] * value
        rhs[slab(z), :] = value
    sides(side_rhs_out.at[1], value)
    own_side = pltpu.make_async_copy(
        side_rhs_out.at[:, pl.ds(my_side, 1)], side_rhs_in.at[:, pl.ds(me, 1)], own_sem.at[3]
    )

    for h, s in enumerate(SIDES):
        target = PLACES[s]

        @pl.when(target != me)
        def _():
            pltpu.make_async_remote_copy(
                side_rhs_out.at[:, pl.ds(h, 1)],
                side_rhs_in.at[:, pl.ds(me, 1)],
                send_sem.at[5],
                recv_sem.at[5],
                device_id=(row, target),
                device_id_type=MESH,
            ).start()

    @pl.when(siding)
    def _():
        own_side.start()

    lines = axial * g_size
    def send_back(first, size, j, carry):
        @pl.when(j != me)
        def _():
            pltpu.make_async_remote_copy(
                edge_out.at[:, pl.ds(j * g_size + first, size)],
                edge_in.at[:, pl.ds(my_solver * g_size + first, size)],
                send_sem.at[4],
                recv_sem.at[4],
                device_id=(row, j),
                device_id_type=MESH,
            ).start()

        return carry

    def send_back_to(start, stop):
        @pl.when(siding)
        def _():
            lax.fori_loop(start, stop, functools.partial(send_back, skipped, kept_size), 0)

        @pl.when(plain)
        def _():
            lax.fori_loop(start, stop, functools.partial(send_back, 0, g_size), 0)

    own_back = pltpu.make_async_copy(
        edge_out.at[:, pl.ds(me * g_size, g_size)],
        edge_in.at[:, pl.ds(my_solver * g_size, g_size)],
        own_sem.at[2],
    )

    @pl.when(solving)
    def _():
        at = lax.broadcasted_iota(jnp.int32, (lines, LANES), 0)

        def down(x, blocks):
            return pltpu.roll(x, blocks * g_size, 0)

        def up(x, blocks):
            return pltpu.roll(x, lines - blocks * g_size, 0)

        is_first = at < g_size
        is_last = at >= lines - g_size
        drain(mat_in, recv_sem.at[2], (axial - 1) * g_size)
        own_matrix.wait()
        low = mat_in[0]
        excess = mat_in[1] + jnp.where(is_last, 1.0, up(mat_in[2], 1))
        high = jnp.where(is_last, 0.0, up(mat_in[3], 1))
        excess = jnp.where(is_first, excess + low, excess)
        low = jnp.where(is_first, 0.0, low)
        level, stride = 0, 1
        while stride < axial:
            inverse = 1.0 / (low + excess + high)
            a = low * down(inverse, stride)
            b = high * up(inverse, stride)
            alpha[level] = a
            beta[level] = b
            excess = excess + a * down(excess, stride) + b * up(excess, stride)
            low = a * down(low, stride)
            high = b * up(high, stride)
            level, stride = level + 1, stride * 2
        final = 1.0 / excess
        finals[...] = final

        by_role(rhs_in, recv_sem.at[3], (axial - 1) * kept_size, (axial - 1) * g_size)
        own_rhs.wait()
        r = rhs_in[0] + jnp.where(is_last, 0.0, up(rhs_in[1], 1))
        level, stride = 0, 1
        while stride < axial:
            r = r + alpha[level] * down(r, stride) + beta[level] * up(r, stride)
            level, stride = level + 1, stride * 2
        r = r * final
        edge_out[1] = r
        edge_out[0] = jnp.where(is_first, 0.0, down(r, 1))

        send_back_to(0, RING_Y)
        own_back.start()

    own_side_back = pltpu.make_async_copy(
        side_edge_out.at[:, pl.ds(me, 1)], side_edge_in.at[:, pl.ds(my_side, 1)], own_sem.at[4]
    )

    @pl.when(siding)
    def _():
        at = lax.broadcasted_iota(jnp.int32, (axial, LANES), 0)

        def down(x, blocks):
            return pltpu.roll(x, blocks, 0)

        def up(x, blocks):
            return pltpu.roll(x, axial - blocks, 0)

        local = (g_size - 1) * (my_side // 2)
        levels = alpha.shape[0]
        for level in range(levels):
            side_alpha[level] = alpha[level, pl.ds(local, axial, stride=g_size), :]
            side_beta[level] = beta[level, pl.ds(local, axial, stride=g_size), :]
        final = finals[pl.ds(local, axial, stride=g_size), :]
        drain(side_rhs_in, recv_sem.at[5], axial - 1)
        own_side.wait()
        r = side_rhs_in[0] + jnp.where(at == axial - 1, 0.0, up(side_rhs_in[1], 1))
        level, stride = 0, 1
        while stride < axial:
            r = r + side_alpha[level] * down(r, stride) + side_beta[level] * up(r, stride)
            level, stride = level + 1, stride * 2
        r = r * final
        side_edge_out[1] = r
        side_edge_out[0] = jnp.where(at == 0, 0.0, down(r, 1))

        def send(j, carry):
            @pl.when(j != me)
            def _():
                pltpu.make_async_remote_copy(
                    side_edge_out.at[:, pl.ds(j, 1)],
                    side_edge_in.at[:, pl.ds(my_side, 1)],
                    send_sem.at[6],
                    recv_sem.at[6],
                    device_id=(row, j),
                    device_id_type=MESH,
                ).start()

            return carry

        lax.fori_loop(0, axial, send, 0)
        own_side_back.start()

    send_back_to(RING_Y, axial)

    @pl.when(siding)
    def _():
        own_side_back.wait()
        drain(side_edge_in, recv_sem.at[6], len(SIDES) - 1)

    @pl.when(jnp.logical_not(siding))
    def _():
        drain(side_edge_in, recv_sem.at[6], len(SIDES))

    by_role(edge_in, recv_sem.at[4], total - kept_size, total - g_size, total)

    @pl.when(solving)
    def _():
        own_back.wait()

    for k in range(2):
        for h, g in enumerate(BESIDE):
            edge_in[k, pl.ds(g, 1), :] = side_edge_in[k, pl.ds(h, 1), :]

    below_edge = gathered(edge_in.at[0])
    own_edge = gathered(edge_in.at[1])
    for z in range(last):
        out_ref[slab(z), :] = (
            rhs[slab(z), :] + below[slab(z), :] * below_edge + above[slab(z), :] * own_edge
        )
    out_ref[slab(last), :] = own_edge

    @pl.when(has_low)
    def _():
        to_low(device_id=(row, me)).wait_send()

    @pl.when(has_high)
    def _():
        to_high(device_id=(row, me)).wait_send()

    by_role(mat_out, send_sem.at[2], axial - g_size, axial - g_size, axial)
    by_role(rhs_out, send_sem.at[3], total - kept_size, total - g_size, total)
    by_role(edge_out, send_sem.at[4], (axial - 1) * kept_size, (axial - 1) * g_size)

    @pl.when(siding)
    def _():
        drain(side_rhs_out, send_sem.at[5], len(SIDES) - 1)
        drain(side_edge_out, send_sem.at[6], axial - 1)

    @pl.when(jnp.logical_not(siding))
    def _():
        drain(side_rhs_out, send_sem.at[5], len(SIDES))


def solution(mesh):
    axial, rows = mesh.shape["axial"], mesh.shape["row"]

    def on_device(warmth, supply, lower, higher, ratio, group, region, sense):
        depth, width, length = warmth.shape
        flat = (depth * width, length)
        lines = axial * (axial // len(PLACES))
        levels = axial.bit_length() - 1
        field = pltpu.VMEM(flat, jnp.float32)
        halo = pltpu.VMEM((depth, length), jnp.float32)
        out = pl.pallas_call(
            functools.partial(kernel, axial, rows, depth),
            out_shape=jax.ShapeDtypeStruct(flat, jnp.float32),
            in_specs=[pl.BlockSpec(memory_space=pltpu.HBM)] * 8,
            out_specs=pl.BlockSpec(memory_space=pltpu.VMEM),
            scratch_shapes=[
                field,
                field,
                field,
                field,
                pltpu.VMEM(group.shape, jnp.int32),
                pltpu.SMEM(ratio.shape, jnp.float32),
                pltpu.SMEM(region.shape, jnp.int32),
                pltpu.SMEM(sense.shape, jnp.int32),
                field,
                field,
                field,
                field,
                field,
                field,
                field,
                field,
                pltpu.VMEM((2, depth, length), jnp.float32),
                halo,
                halo,
                pltpu.VMEM((4, axial, LANES), jnp.float32),
                pltpu.VMEM((4, lines, LANES), jnp.float32),
                pltpu.VMEM((2, axial, LANES), jnp.float32),
                pltpu.VMEM((2, lines, LANES), jnp.float32),
                pltpu.VMEM((2, lines, LANES), jnp.float32),
                pltpu.VMEM((2, axial, LANES), jnp.float32),
                pltpu.VMEM((2, len(SIDES), LANES), jnp.float32),
                pltpu.VMEM((2, axial, LANES), jnp.float32),
                pltpu.VMEM((2, axial, LANES), jnp.float32),
                pltpu.VMEM((2, len(SIDES), LANES), jnp.float32),
                pltpu.VMEM((levels, lines, LANES), jnp.float32),
                pltpu.VMEM((levels, lines, LANES), jnp.float32),
                pltpu.VMEM((levels, axial, LANES), jnp.float32),
                pltpu.VMEM((levels, axial, LANES), jnp.float32),
                pltpu.VMEM((lines, LANES), jnp.float32),
                pltpu.SemaphoreType.DMA((5,)),
                pltpu.SemaphoreType.DMA((3,)),
                pltpu.SemaphoreType.DMA((5,)),
                pltpu.SemaphoreType.DMA((7,)),
                pltpu.SemaphoreType.DMA((7,)),
            ],
            compiler_params=pltpu.CompilerParams(
                collective_id=0, has_side_effects=True, vmem_limit_bytes=32 * 1024 * 1024
            ),
        )(
            *(
                pltpu.with_memory_space_constraint(x, pltpu.HBM)
                for x in (
                    warmth.reshape(flat),
                    supply.reshape(flat),
                    lower.reshape(flat),
                    higher.reshape(flat),
                    ratio,
                    group,
                    region,
                    sense,
                )
            )
        )
        return out.reshape(warmth.shape)

    placed = (
        P("axial", "row", None),
        P("axial", "row", None),
        P("axial", "row", None),
        P("axial", "row", None),
        P(),
        P("row", None),
        P("axial"),
        P(),
    )
    return jax.shard_map(
        on_device, mesh=mesh, in_specs=placed, out_specs=P("axial", "row", None), check_vma=False
    )
```
